128 devices in a mesh: tm: 32 (over z_lo, y, x), head: 4 (over z_hi, core).
Axes of the slice: x: 4, y: 4, z: 4 (z_hi: 2, z_lo: 2; z = z_hi * 2 + z_lo), core: 2. Of those that a mesh axis runs over, the one named last changes fastest.
Arguments:
- query: bfloat16 [16384, 2560], P('tm', 'head'), may hold values from -5 to 5
- key: bfloat16 [16384, 2560], P('tm', 'head'), may hold values from -5 to 5
- value: bfloat16 [16384, 2560], P('tm', 'head'), may hold values from -6 to 6
- out_weight: bfloat16 [2560, 5120], P('head'), may hold values from -0.125 to 0.125
- grad_out: bfloat16 [16384, 5120], P('tm', 'head'), may hold values from -6 to 6
- sink_frame: int32 [20], P('head'), may hold values from 0 to 1
- window: int32 [20], P('head'), may hold values from 1 to 3
Outputs:
- grad_query: bfloat16 [16384, 2560], P('tm', 'head')
- grad_key: bfloat16 [16384, 2560], P('tm', 'head')
- grad_value: bfloat16 [16384, 2560], P('tm', 'head')
- grad_weight: float32 [2560, 5120], P('head', 'tm')
The draws below stay inside these ranges and needn't reach their ends.
All inputs are finite; a program needn't handle non-finite values.
Results may differ from the reference program's by a relative error of at most 0.0077.
Values may be sent and summed in bfloat16 or wider, within the bound.
A program may use at most 192 MiB of HBM per device.

```python
import math
import jax
import jax.numpy as jnp
from jax import lax

D = 5120
HEADS = 20
HD = 128
TPF = 256
FR_DEV = 2
WMAX = 3
FRAMES = 64
TOKENS = 16384


def paired_fields(key):
    shape = (TOKENS, HEADS * HD)
    base_query = jnp.clip(jax.random.normal(jax.random.fold_in(key, 21), shape, jnp.float32), -5.0, 5.0)
    base_key = jnp.clip(jax.random.normal(jax.random.fold_in(key, 22), shape, jnp.float32), -5.0, 5.0)
    row_ids = jnp.arange(TOKENS, dtype=jnp.int32)
    position = row_ids % TPF
    leading = (position % 64 == 7)[:, None]
    trailing = (position % 64 == 8)[:, None]
    query_field = jnp.where(leading, base_query, base_query)
    key_field = jnp.where(leading, base_key, jnp.where(trailing, base_key, base_key))
    return (query_field.astype(jnp.bfloat16), key_field.astype(jnp.bfloat16))


def draw_query(key, part):
    query_field, key_field = paired_fields(key)
    return query_field


def draw_key(key, part):
    query_field, key_field = paired_fields(key)
    return key_field


def draw_window(key, part):
    key = jax.random.fold_in(key, 3)
    spans = jax.random.randint(jax.random.fold_in(key, 1), (HEADS,), 1, WMAX + 1)
    order = jax.random.permutation(jax.random.fold_in(key, 2), HEADS)
    spans = spans.at[order[0]].set(WMAX)
    spans = spans.at[order[1]].set(1)
    return spans.astype(jnp.int32)


def draw_sink_frame(key, part):
    key = jax.random.fold_in(key, 5)
    chosen = jax.random.randint(jax.random.fold_in(key, 1), (HEADS,), 0, FR_DEV)
    order = jax.random.permutation(jax.random.fold_in(key, 2), HEADS)
    chosen = chosen.at[order[0]].set(FR_DEV - 1)
    chosen = chosen.at[order[1]].set(0)
    return chosen.astype(jnp.int32)


def raised(array, rng, source, target, shards_of, factor):
    def block_of(dim):
        return (jnp.arange(array.shape[dim]) // (array.shape[dim] // shards_of)).reshape((-1,) + (1,) * (array.ndim - 1 - dim))

    first = jax.random.permutation(rng, shards_of)[block_of(target)]
    second = (block_of(target) + shards_of // 2) % shards_of
    return jnp.where((block_of(source) == first) | (block_of(source) == second), factor * array, array)


def steps_of(key, shape, cuts, smallest, largest):
    level = 1.0
    for axis_at, blocks in cuts:
        steps = jax.random.uniform(jax.random.fold_in(jax.random.fold_in(key, 6), axis_at), (blocks,), jnp.float32, smallest / len(cuts), largest / len(cuts))
        level = level * jnp.repeat(jnp.exp(steps), shape[axis_at] // blocks).reshape((-1,) + (1,) * (len(shape) - 1 - axis_at))
    return level


def normal_values(key, dims, spread, limit, shards=(), held_as=jnp.bfloat16):
    values = spread * jax.random.normal(key, dims, jnp.float32)
    if shards:
        values = values * steps_of(key, dims, shards, -0.22, 0.18)
    return jnp.clip(values, -limit, limit).astype(held_as)


def bell_draw_with(own_key, dims, scale, most, shards, heavy, kind=jnp.bfloat16):
    entries = scale * jax.random.normal(own_key, dims, jnp.float32)
    if shards:
        entries = entries * steps_of(own_key, dims, shards, -0.22, 0.18)
    return jnp.clip(raised(entries, jax.random.fold_in(own_key, 3), *heavy), -most, most).astype(kind)


def setup_inputs(seed: int = 0) -> dict:
    key_list = jax.random.split(jax.random.key(seed), 8)
    return {
        "query": draw_query(jax.random.fold_in(key_list[7], 71), 0),
        "key": draw_key(jax.random.fold_in(key_list[7], 71), 0),
        "value": normal_values(key_list[2], (TOKENS, HEADS * HD), 1.0, 6.0, ((0, 32), (1, 4))),
        "out_weight": normal_values(key_list[3], (HEADS * HD, D), (HEADS * HD) ** -0.5, 0.125, ((0, 4),)),
        "grad_out": bell_draw_with(key_list[4], (TOKENS, D), 1.0, 6.0, ((0, 32), (1, 4)), (0, 1, 32, 2.75)),
        "sink_frame": draw_sink_frame(jax.random.fold_in(key_list[7], 71), 0),
        "window": draw_window(jax.random.fold_in(key_list[7], 71), 0),
    }


def reference(query, key, value, out_weight, grad_out, sink_frame, window):
    scale = 1.0 / math.sqrt(HD)
    width = HEADS * HD
    margin = WMAX - 1
    queries = query.astype(jnp.float32).reshape(FRAMES, TPF, HEADS, HD)
    keys = key.astype(jnp.float32).reshape(FRAMES, TPF, HEADS, HD)
    values = value.astype(jnp.float32).reshape(FRAMES, TPF, HEADS, HD)
    cotangent = grad_out.reshape(FRAMES, TPF, D)
    weight_rows = out_weight.T
    frame_ids = jnp.arange(FRAMES, dtype=jnp.int32)
    choose = (frame_ids[:, None] == sink_frame[None, :]).astype(jnp.float32)
    sink_keys = jnp.einsum('fh,fphd->phd', choose, keys)
    sink_values = jnp.einsum('fh,fphd->phd', choose, values)
    padding = jnp.zeros((margin, TPF, HEADS, HD), jnp.float32)
    keys_pad = jnp.concatenate((padding, keys), axis=0)
    values_pad = jnp.concatenate((padding, values), axis=0)
    slots = jnp.arange(WMAX, dtype=jnp.int32)

    def advance(carry, frame):
        key_grad, value_grad, weight_grad = carry
        here = lax.dynamic_index_in_dim(queries, frame, 0, keepdims=False)
        near_keys = lax.dynamic_slice_in_dim(keys_pad, frame, WMAX, 0).reshape(WMAX * TPF, HEADS, HD)
        near_values = lax.dynamic_slice_in_dim(values_pad, frame, WMAX, 0).reshape(WMAX * TPF, HEADS, HD)
        near_keys = jnp.concatenate((near_keys, sink_keys), axis=0)
        near_values = jnp.concatenate((near_values, sink_values), axis=0)
        key_frames = frame - margin + slots
        reach = frame - window
        window_seen = (key_frames[None, :] >= 0) & (key_frames[None, :] > reach[:, None])
        visible = jnp.concatenate((window_seen, (sink_frame <= reach)[:, None]), axis=1)
        visible = jnp.repeat(visible, TPF, axis=1)[:, None, :]
        scores = jnp.einsum('qhd,khd->hqk', here, near_keys) * scale
        masked = jnp.where(visible, scores, -1e+30)
        peak = lax.optimization_barrier(jnp.max(masked, axis=2, keepdims=True))
        weights = jnp.exp(masked - peak)
        probs = weights / lax.optimization_barrier(jnp.sum(weights, axis=2, keepdims=True))
        probs_low = lax.optimization_barrier(probs.astype(jnp.bfloat16)).astype(jnp.float32)
        attended = jnp.einsum('hqk,khd->qhd', probs_low, near_values).reshape(TPF, width).astype(jnp.bfloat16)
        out_rows = lax.dynamic_index_in_dim(cotangent, frame, 0, keepdims=False)
        grad_att = jnp.dot(out_rows, weight_rows, preferred_element_type=jnp.float32).astype(jnp.bfloat16)
        weight_grad = weight_grad + jnp.dot(attended.T, out_rows, preferred_element_type=jnp.float32)
        grad_heads = lax.optimization_barrier(grad_att).astype(jnp.float32).reshape(TPF, HEADS, HD)
        grad_probs = jnp.einsum('qhd,khd->hqk', grad_heads, near_values)
        delta = lax.optimization_barrier(jnp.sum(probs * grad_probs, axis=2, keepdims=True))
        grad_scores = (probs * (grad_probs - delta) * scale).astype(jnp.bfloat16)
        grad_scores = lax.optimization_barrier(grad_scores).astype(jnp.float32)
        grad_query = jnp.einsum('hqk,khd->qhd', grad_scores, near_keys).reshape(TPF, width).astype(jnp.bfloat16)
        grad_near = jnp.einsum('hqk,qhd->khd', grad_scores, here)[:WMAX * TPF].reshape(WMAX, TPF, HEADS, HD)
        grad_near_values = jnp.einsum('hqk,qhd->khd', probs_low, grad_heads)[:WMAX * TPF].reshape(WMAX, TPF, HEADS, HD)
        key_grad = lax.dynamic_update_slice_in_dim(key_grad, lax.dynamic_slice_in_dim(key_grad, frame, WMAX, 0) + grad_near, frame, 0)
        value_grad = lax.dynamic_update_slice_in_dim(value_grad, lax.dynamic_slice_in_dim(value_grad, frame, WMAX, 0) + grad_near_values, frame, 0)
        return ((key_grad, value_grad, weight_grad), grad_query)
    start = (jnp.zeros((FRAMES + margin, TPF, HEADS, HD), jnp.float32), jnp.zeros((FRAMES + margin, TPF, HEADS, HD), jnp.float32), jnp.zeros((width, D), jnp.float32))
    (key_grad, value_grad, weight_grad), grad_query = lax.scan(advance, start, frame_ids)
    grad_query = grad_query.reshape(TOKENS, width)
    grad_key = key_grad[margin:].reshape(TOKENS, width).astype(jnp.bfloat16)
    grad_value = value_grad[margin:].reshape(TOKENS, width).astype(jnp.bfloat16)
    return (grad_query, grad_key, grad_value, weight_grad)
```

```python
import math

import jax
import jax.numpy as jnp
from jax import lax
from jax.experimental import pallas as pl
from jax.experimental.pallas import tpu as pltpu
from jax.sharding import PartitionSpec as P

MESH = pl.DeviceIdType.MESH
BF = jnp.bfloat16
F32 = jnp.float32
NT = 32
H = 5
HD = 128
T = 256
L = 2 * T
SCALE = 1.0 / math.sqrt(HD)
SCALE2 = SCALE * math.log2(math.e)
CW = 1280
GC = 4
YB = 640
XB = 160
LAST = ((1,), (1,))


def mm(a, b):
    return lax.dot_general(a, b, (((1,), (0,)), ((), ())), preferred_element_type=F32)


def mmt(a, b):
    return lax.dot_general(a, b, (LAST, ((), ())), preferred_element_type=F32)


def kernel(
    q_ref, k_ref, v_ref, w_ref, g_ref, sink_ref, win_ref,
    dq_ref, dk_ref, dv_ref, wo_ref,
    Q, KV, SB, RB, COT, COTT, W, GA, DO, PR, ATT, YS, YR, YSUM, XS, XR, XK, ZF, ZS, ZR, WO,
    DPS, DPR, DQ, DKV,
    l_sem, w_sem, kv_s, kv_r, zg_s, zg_r, co_s, co_r, cf_s, cf_r, sc_s, sc_r, ag_s, ag_r,
    y_s, y_r, x_s, x_r, z_s, z_r, d_s, d_r, o_sem,
):
    t = lax.axis_index("tm")
    hd = lax.axis_index("head")
    zl, y, x = t // 16, (t // 4) % 4, t % 4
    zh, core = hd // 2, hd % 2
    mate = hd + 1 - 2 * core
    far = (hd + 2) % 4
    far_mate = (mate + 2) % 4

    def remote(src, dst, ss, rs, dev):
        return pltpu.make_async_remote_copy(
            src_ref=src, dst_ref=dst, send_sem=ss, recv_sem=rs, device_id=dev, device_id_type=MESH
        )

    def load_own(n):
        ref = (k_ref, v_ref)[n // H] if n < 2 * H else q_ref
        h = n % H
        dst = KV.at[n // H, h, pl.ds(L, L)] if n < 2 * H else Q.at[h]
        return pltpu.make_async_copy(ref.at[:, pl.ds(h * HD, HD)], dst, l_sem.at[n])

    def load_w(s):
        return pltpu.make_async_copy(w_ref.at[:, pl.ds(s * CW, CW)], W.at[s], w_sem.at[s])

    load_g = pltpu.make_async_copy(g_ref, COT.at[hd], w_sem.at[4])
    for n in range(3 * H):
        load_own(n).start()
    load_g.start()
    for s in range(4):
        load_w(s).start()

    barrier = pltpu.get_barrier_semaphore()

    def greet(i, _):
        pl.semaphore_signal(barrier, inc=1, device_id=((t + i) % NT, hd), device_id_type=MESH)
        return 0

    lax.fori_loop(1, NT, greet, 0)
    pl.semaphore_signal(barrier, inc=1, device_id=(t, mate), device_id_type=MESH)
    pl.semaphore_signal(barrier, inc=1, device_id=(t, far), device_id_type=MESH)
    pl.semaphore_wait(barrier, NT + 1)

    def kv_copy(n, h):
        ref = (k_ref, v_ref)[n]
        return remote(
            ref.at[:, pl.ds(h * HD, HD)], KV.at[n, h, pl.ds(0, L)],
            kv_s.at[n, h], kv_r.at[n, h], ((t + 1) % NT, hd),
        )

    def zg_copy(r):
        rows = pl.ds(r * (L // GC), L // GC)
        return remote(g_ref.at[rows], COT.at[hd, rows], zg_s.at[r], zg_r.at[r], (t, far))

    def zg_wait(r):
        rows = pl.ds(r * (L // GC), L // GC)
        remote(COT.at[far, rows], COT.at[far, rows], zg_s.at[r], zg_r.at[r], (t, far)).wait_recv()

    def cf_copy(r):
        rows = pl.ds(r * (L // GC), L // GC)
        return remote(COT.at[far, rows], COT.at[far, rows], cf_s.at[r], cf_r.at[r], (t, mate))

    def cf_wait(r):
        rows = pl.ds(r * (L // GC), L // GC)
        remote(
            COT.at[far_mate, rows], COT.at[far_mate, rows], cf_s.at[r], cf_r.at[r], (t, mate)
        ).wait_recv()

    co_copy = remote(g_ref, COT.at[hd], co_s, co_r, (t, mate))
    co_arrival = remote(COT.at[mate], COT.at[mate], co_s, co_r, (t, mate))

    co_copy.start()
    for r in range(GC):
        zg_copy(r).start()
    for h in range(H):
        kv_copy(0, h).start()
        kv_copy(1, h).start()

    def piece(buf, i):
        return buf.at[i // 16, :, pl.ds(pl.multiple_of((i % 16) * 16, 16), 16), :]

    for n in range(3 * H):
        load_own(n).wait()

    @pl.when(t == 0)
    def _():
        for h in range(H):
            second = sink_ref[h].astype(F32)
            for n in range(2):
                a = KV[n, h, pl.ds(L, T)].astype(F32)
                b = KV[n, h, pl.ds(L + T, T)].astype(F32)
                RB[n, h] = (a * (1.0 - second) + b * second).astype(BF)
        SB[0, :, pl.ds(0, 16), :] = RB[0, :, pl.ds(0, 16), :]

        def scatter(i, _):
            remote(piece(RB, i), piece(SB, i), sc_s.at[i], sc_r, (i, hd)).start()
            return 0

        lax.fori_loop(1, NT, scatter, 0)

    @pl.when(t != 0)
    def _():
        remote(piece(SB, t), piece(SB, t), sc_s.at[0], sc_r, (0, hd)).wait_recv()

    def ag_copy(i):
        return remote(piece(SB, t), piece(SB, t), ag_s.at[i], ag_r.at[t], ((t + i) % NT, hd))

    def ag_start(i, _):
        ag_copy(i).start()
        return 0

    lax.fori_loop(1, NT, ag_start, 0)

    def use_block(s, first):
        for half in range(2):
            COTT[2 * s + half] = COT[s, :, pl.ds(half * YB, YB)].T

        def rows(m, _):
            at = pl.ds(pl.multiple_of(m * 128, 128), 128)
            got = mmt(COT[s, at], W[s])
            GA[at] = got if first else GA[at] + got
            return 0

        lax.fori_loop(0, L // 128, rows, 0)

    load_g.wait()
    for s in range(4):
        load_w(s).wait()
    use_block(hd, True)
    co_arrival.wait_recv()
    use_block(mate, False)

    def ag_wait(i, _):
        src = (t + i) % NT
        remote(piece(SB, src), piece(SB, src), ag_s.at[i], ag_r.at[src], (src, hd)).wait_recv()
        return 0

    lax.fori_loop(1, NT, ag_wait, 0)

    def biases(h, i):
        f = 2 * t + i
        win, snk = win_ref[h], sink_ref[h]
        off = jnp.float32(-1e30)
        on = jnp.float32(0.0)
        return (
            jnp.where((win >= 3) & (f >= 2), on, off),
            jnp.where((win >= 2) & (f >= 1), on, off),
            None,
            jnp.where(snk <= f - win, on, off),
        )

    def forward(h):
        vt = KV[1, h].T
        svt = SB[1, h].T
        for i in range(2):
            q = Q[h, pl.ds(i * T, T)]
            peak = None
            scores = []
            for b, bias in enumerate(biases(h, i)):
                keys = KV[0, h, pl.ds((i + b) * T, T)] if b < 3 else SB[0, h]
                s = mmt(keys, q) * SCALE2
                if bias is not None:
                    s = s + bias
                top = jnp.max(s, axis=0, keepdims=True)
                peak = top if peak is None else jnp.maximum(peak, top)
                scores.append(s)
            weights = [jnp.exp2(s - peak) for s in scores]
            total = sum(jnp.sum(e, axis=0, keepdims=True) for e in weights)
            inverse = 1.0 / total
            out = None
            for b, e in enumerate(weights):
                p = e * inverse
                PR[2 * h + i, pl.ds(b * T, T)] = p
                values = vt[:, (i + b) * T : (i + b + 1) * T] if b < 3 else svt
                term = mm(values, p.astype(BF))
                out = term if out is None else out + term
            ATT[h, :, pl.ds(i * T, T)] = out.astype(BF)

    def d_copy(h):
        return remote(DPS.at[h], DPR.at[h], d_s.at[h], d_r.at[h], ((t + NT - 1) % NT, hd))

    def out_copy(n, h):
        ref = (dq_ref, dk_ref, dv_ref)[n]
        src = DQ.at[h] if n == 0 else DKV.at[n - 1, h]
        return pltpu.make_async_copy(src, ref.at[:, pl.ds(pl.multiple_of(h * HD, HD), HD)], o_sem.at[n, h])

    def backward(h):
        kt = KV[0, h].T
        skt = SB[0, h].T
        near = []
        for i in range(2):
            q = Q[h, pl.ds(i * T, T)]
            do = DO[h, pl.ds(i * T, T)]
            grads = []
            delta = None
            for b in range(4):
                values = KV[1, h, pl.ds((i + b) * T, T)] if b < 3 else SB[1, h]
                dp = mmt(values, do)
                term = jnp.sum(PR[2 * h + i, pl.ds(b * T, T)] * dp, axis=0, keepdims=True)
                delta = term if delta is None else delta + term
                grads.append(dp)
            out = None
            terms = []
            for b in range(4):
                p = PR[2 * h + i, pl.ds(b * T, T)]
                ds = (p * (grads[b] - delta) * SCALE).astype(BF)
                keys = kt[:, (i + b) * T : (i + b + 1) * T] if b < 3 else skt
                term = mm(keys, ds)
                out = term if out is None else out + term
                if b < 3:
                    terms.append((mm(ds, q), mm(p.astype(BF), do)))
            DQ[h, pl.ds(i * T, T)] = out.T.astype(BF)
            near.append(terms)
        out_copy(0, h).start()
        for n in range(2):
            DPS[h, n, pl.ds(0, T)] = near[0][0][n].astype(BF)
            DPS[h, n, pl.ds(T, T)] = (near[0][1][n] + near[1][0][n]).astype(BF)
            PR[2 * h, pl.ds(0, T), pl.ds(n * HD, HD)] = near[0][2][n] + near[1][1][n]
            PR[2 * h, pl.ds(T, T), pl.ds(n * HD, HD)] = near[1][2][n]
        d_copy(h).start()

    def finish_kv(h):
        d_copy(h).wait_recv()
        for n in range(2):
            own = PR[2 * h, pl.ds(0, L), pl.ds(n * HD, HD)]
            DKV[n, h] = (own + DPR[h, n].astype(F32)).astype(BF)
            out_copy(n + 1, h).start()

    def which(j):
        g = (zh + j // H) % 2
        h = j % H
        return g, h, 1 - 2 * ((g + h) % 2)

    def part(g, yy, h):
        return mmt(COTT[g * 4 + yy], ATT[h])

    def y_copy(j, m):
        _, _, d = which(j)
        to = (y + (d if m != 1 else -d) + 4) % 4
        return remote(YS.at[j, m], YR.at[j, m], y_s.at[j, m], y_r.at[j, m], (zl * 16 + to * 4 + x, hd))

    def x_copy(j, m):
        _, _, d = which(j)
        to = (x + (d if m != 1 else -d) + 4) % 4
        return remote(XS.at[j, m], XR.at[j, m], x_s.at[j, m], x_r.at[j, m], (zl * 16 + y * 4 + to, hd))

    def z_copy(h):
        return remote(ZS.at[h], ZR.at[h], z_s.at[h], z_r.at[h], ((t + 16) % NT, hd))

    def step1(j):
        g, h, d = which(j)
        YS[j, 0] = part(g, (y + 2) % 4, h).astype(BF)
        y_copy(j, 0).start()
        YS[j, 1] = part(g, (y - d + 4) % 4, h).astype(BF)
        y_copy(j, 1).start()

    def step2(j):
        g, h, d = which(j)
        own = part(g, (y + d + 4) % 4, h)
        y_copy(j, 0).wait_recv()
        YS[j, 2] = (own + YR[j, 0].astype(F32)).astype(BF)
        y_copy(j, 2).start()

    def x_rows(xx):
        return pl.ds(pl.multiple_of(xx * XB, XB), XB)

    def step3(j):
        g, h, d = which(j)
        own = part(g, y, h)
        y_copy(j, 1).wait_recv()
        y_copy(j, 2).wait_recv()
        YSUM[...] = own + YR[j, 1].astype(F32) + YR[j, 2].astype(F32)
        XS[j, 0] = YSUM[x_rows((x + 2) % 4)].astype(BF)
        x_copy(j, 0).start()
        XS[j, 1] = YSUM[x_rows((x - d + 4) % 4)].astype(BF)
        x_copy(j, 1).start()
        XK[j, 0] = YSUM[x_rows((x + d + 4) % 4)]
        XK[j, 1] = YSUM[x_rows(x)]

    def step4(j):
        x_copy(j, 0).wait_recv()
        XS[j, 2] = (XK[j, 0] + XR[j, 0].astype(F32)).astype(BF)
        x_copy(j, 2).start()

    def step5(j):
        g, h, _ = which(j)
        x_copy(j, 1).wait_recv()
        x_copy(j, 2).wait_recv()
        ZF[g, h] = XK[j, 1] + XR[j, 1].astype(F32) + XR[j, 2].astype(F32)

        @pl.when(j >= H)
        def _():
            ZS[h] = ZF[1 - zl, h].astype(BF)
            z_copy(h).start()

    def step6(h):
        z_copy(h).wait_recv()
        WO[h] = ZF[zl, h] + ZR[h].astype(F32)

    def turn(j, _):
        @pl.when(j < GC)
        def _():
            zg_wait(j)
            cf_copy(j).start()

        @pl.when(j < H)
        def _():
            for n in range(2):
                remote(
                    KV.at[n, j, pl.ds(0, L)], KV.at[n, j, pl.ds(0, L)],
                    kv_s.at[n, j], kv_r.at[n, j], ((t + 1) % NT, hd),
                ).wait_recv()
            forward(j)

        @pl.when(j == H)
        def _():
            use_block(far, False)
            for r in range(GC):
                cf_wait(r)
            use_block(far_mate, False)
            for h in range(H):
                DO[h] = GA[:, h * HD : (h + 1) * HD].astype(BF)

        @pl.when(j < 2 * H)
        def _():
            step1(j)

        @pl.when((j >= 1) & (j < 2 * H + 1))
        def _():
            step2(j - 1)

        @pl.when((j >= H) & (j < 2 * H))
        def _():
            backward(j - H)

        @pl.when((j >= 2) & (j < 2 * H + 2))
        def _():
            step3(j - 2)

        @pl.when((j >= 3) & (j < 2 * H + 3))
        def _():
            step4(j - 3)

        @pl.when((j >= H + 2) & (j < 2 * H + 2))
        def _():
            finish_kv(j - H - 2)

        @pl.when((j >= 4) & (j < 2 * H + 4))
        def _():
            step5(j - 4)

        @pl.when(j >= H + 5)
        def _():
            step6(j - H - 5)

        return 0

    lax.fori_loop(0, 2 * H + 5, turn, 0)
    put_w = pltpu.make_async_copy(WO, wo_ref, w_sem.at[4])
    put_w.start()

    co_copy.wait_send()
    for r in range(GC):
        zg_copy(r).wait_send()
        cf_copy(r).wait_send()

    @pl.when(t == 0)
    def _():
        def sent(i, _):
            remote(piece(RB, i), piece(SB, i), sc_s.at[i], sc_r, (i, hd)).wait_send()
            return 0

        lax.fori_loop(1, NT, sent, 0)

    def ag_sent(i, _):
        ag_copy(i).wait_send()
        return 0

    lax.fori_loop(1, NT, ag_sent, 0)

    def rs_sent(j, _):
        for m in range(3):
            y_copy(j, m).wait_send()
            x_copy(j, m).wait_send()
        return 0

    lax.fori_loop(0, 2 * H, rs_sent, 0)
    for h in range(H):
        kv_copy(0, h).wait_send()
        kv_copy(1, h).wait_send()
        z_copy(h).wait_send()
        d_copy(h).wait_send()
        for n in range(3):
            out_copy(n, h).wait()
    put_w.wait()


def per_device(query, key, value, out_weight, grad_out, sink_frame, window):
    dma = pltpu.SemaphoreType.DMA
    any_spec = pl.BlockSpec(memory_space=pl.ANY)
    smem = pl.BlockSpec(memory_space=pltpu.SMEM)
    sds = jax.ShapeDtypeStruct
    grad_query, grad_key, grad_value, weight = pl.pallas_call(
        kernel,
        out_shape=[sds((L, H * HD), BF)] * 3 + [sds((H, XB, HD), F32)],
        in_specs=[any_spec] * 5 + [smem] * 2,
        out_specs=[any_spec] * 4,
        scratch_shapes=[
            pltpu.VMEM((H, L, HD), BF),
            pltpu.VMEM((2, H, 2 * L, HD), BF),
            pltpu.VMEM((2, H, T, HD), BF),
            pltpu.VMEM((2, H, T, HD), BF),
            pltpu.VMEM((4, L, CW), BF),
            pltpu.VMEM((8, YB, L), BF),
            pltpu.VMEM((4, H * HD, CW), BF),
            pltpu.VMEM((L, H * HD), F32),
            pltpu.VMEM((H, L, HD), BF),
            pltpu.VMEM((2 * H, 4 * T, T), F32),
            pltpu.VMEM((H, HD, L), BF),
            pltpu.VMEM((2 * H, 3, YB, HD), BF),
            pltpu.VMEM((2 * H, 3, YB, HD), BF),
            pltpu.VMEM((YB, HD), F32),
            pltpu.VMEM((2 * H, 3, XB, HD), BF),
            pltpu.VMEM((2 * H, 3, XB, HD), BF),
            pltpu.VMEM((2 * H, 2, XB, HD), F32),
            pltpu.VMEM((2, H, XB, HD), F32),
            pltpu.VMEM((H, XB, HD), BF),
            pltpu.VMEM((H, XB, HD), BF),
            pltpu.VMEM((H, XB, HD), F32),
            pltpu.VMEM((H, 2, L, HD), BF),
            pltpu.VMEM((H, 2, L, HD), BF),
            pltpu.VMEM((H, L, HD), BF),
            pltpu.VMEM((2, H, L, HD), BF),
            dma((3 * H,)), dma((5,)),
            dma((2, H)), dma((2, H)),
            dma((GC,)), dma((GC,)),
            dma, dma,
            dma((GC,)), dma((GC,)),
            dma((NT,)), dma,
            dma((NT,)), dma((NT,)),
            dma((2 * H, 3)), dma((2 * H, 3)),
            dma((2 * H, 3)), dma((2 * H, 3)),
            dma((H,)), dma((H,)),
            dma((H,)), dma((H,)),
            dma((3, H)),
        ],
        compiler_params=pltpu.CompilerParams(
            collective_id=0, has_side_effects=True, vmem_limit_bytes=60 * 1024 * 1024
        ),
        name="layer_backward",
    )(query, key, value, out_weight, grad_out, sink_frame, window)
    grad_weight = jnp.swapaxes(weight, 1, 2).reshape(H * HD, XB)
    return (grad_query, grad_key, grad_value, grad_weight)


def solution(mesh):
    placed = (
        P("tm", "head"),
        P("tm", "head"),
        P("tm", "head"),
        P("head", None),
        P("tm", "head"),
        P("head"),
        P("head"),
    )
    return jax.shard_map(
        per_device,
        mesh=mesh,
        in_specs=placed,
        out_specs=(P("tm", "head"), P("tm", "head"), P("tm", "head"), P("head", "tm")),
        check_vma=False,
    )
```

```python
import math

import jax
import jax.numpy as jnp
from jax import lax
from jax.experimental import pallas as pl
from jax.experimental.pallas import tpu as pltpu
from jax.sharding import PartitionSpec as P

MESH = pl.DeviceIdType.MESH
BF = jnp.bfloat16
F32 = jnp.float32
NP = 16
NT = 32
H = 5
HD = 128
T = 256
L = 2 * T
SCALE = 1.0 / math.sqrt(HD)
SCALE2 = SCALE * math.log2(math.e)
CW = 1280
GC = 4
YB = 640
XB = 160
LAST = ((1,), (1,))
EARLY_ZG = 0
Z_RELAY = {1: 17, 2: 20, 3: 28, 4: 19}
X_FIRST = (1, 3)
EARLY_PLUS = 3


def mm(a, b):
    return lax.dot_general(a, b, (((1,), (0,)), ((), ())), preferred_element_type=F32)


def mmt(a, b):
    return lax.dot_general(a, b, (LAST, ((), ())), preferred_element_type=F32)


def kernel(
    q_ref, k_ref, v_ref, w_ref, g_ref, sink_ref, win_ref,
    dq_ref, dk_ref, dv_ref, wo_ref,
    Q, KV, SB, RB, RL, RLD, COT, COTT, W, GA, PR, ATT, YS, YR, YSUM, XS, XR, XK, ZF, ZS, ZR, WO,
    DPS, DPR, DQ, DKV,
    l_sem, w_sem, kv_s, kv_r, rl_r, rl_s, rd_r, rd_s, zg_s, zg_r, co_s, co_r, cf_s, cf_r, sc_s, sc_r, ag_s, ag_r,
    y_s, y_r, x_s, x_r, z_s, z_r, d_s, d_r, o_sem,
):
    t = lax.axis_index("tm")
    hd = lax.axis_index("head")
    zl, y, x = t // 16, (t // 4) % 4, t % 4
    zh, core = hd // 2, hd % 2
    mate = hd + 1 - 2 * core
    far = (hd + 2) % 4
    far_mate = (mate + 2) % 4

    def remote(src, dst, ss, rs, dev):
        return pltpu.make_async_remote_copy(
            src_ref=src, dst_ref=dst, send_sem=ss, recv_sem=rs, device_id=dev, device_id_type=MESH
        )

    def load_own(n):
        ref = (k_ref, v_ref)[n // H] if n < 2 * H else q_ref
        h = n % H
        dst = KV.at[n // H, h, pl.ds(L, L)] if n < 2 * H else Q.at[h]
        return pltpu.make_async_copy(ref.at[:, pl.ds(h * HD, HD)], dst, l_sem.at[n])

    def load_w(s):
        return pltpu.make_async_copy(w_ref.at[:, pl.ds(s * CW, CW)], W.at[s], w_sem.at[s])

    load_g = pltpu.make_async_copy(g_ref, COT.at[hd], w_sem.at[4])
    for n in range(3 * H):
        load_own(n).start()
    load_g.start()
    for s in range(4):
        load_w(s).start()

    barrier = pltpu.get_barrier_semaphore()

    def greet(i, _):
        pl.semaphore_signal(barrier, inc=1, device_id=((t + i) % NT, hd), device_id_type=MESH)
        return 0

    lax.fori_loop(1, NT, greet, 0)
    pl.semaphore_signal(barrier, inc=1, device_id=(t, mate), device_id_type=MESH)
    pl.semaphore_signal(barrier, inc=1, device_id=(t, far), device_id_type=MESH)
    pl.semaphore_wait(barrier, NT + 1)

    row_end = (x == 3) & (y < 3)
    plane_end = t == NT // 2 - 1
    row_relay = (x == 3) & (y > 0)

    def kv_copies(n, h):
        src = (k_ref, v_ref)[n].at[:, pl.ds(h * HD, HD)]
        sem = kv_s.at[n, h]
        out = []
        direct = t < NT - 1
        if h >= 3:
            out.append((row_end, remote(src, RL.at[h - 3, n], sem, rl_r.at[h - 3, n], (t + 4, hd))))
            direct = direct & jnp.logical_not(row_end)
        if h in Z_RELAY:
            to = Z_RELAY[h]
            out.append((plane_end, remote(src, RL.at[0, n], sem, rl_r.at[0, n], (to, hd))))
            direct = direct & jnp.logical_not(plane_end)
        place = KV.at[n, h, pl.ds(0, L)]
        out.append((direct, remote(src, place, sem, kv_r.at[n, h], ((t + 1) % NT, hd))))
        return out

    def kv_relays():
        roles = [(row_relay, 0, 3, (t + NT - 3) % NT, 1), (row_relay, 1, 4, (t + NT - 3) % NT, 2)]
        roles += [(t == at, 0, h, NT // 2, h - 1) for h, at in Z_RELAY.items()]
        for mine, slot, h, to, turn in roles:
            for n in range(2):
                yield turn, mine, remote(
                    RL.at[slot, n], KV.at[n, h, pl.ds(0, L)], rl_s.at[slot, n], kv_r.at[n, h], (to, hd)
                ), remote(RL.at[slot, n], RL.at[slot, n], rl_s.at[slot, n], rl_r.at[slot, n], (to, hd))

    def when(condition, act):
        @pl.when(condition)
        def _():
            act()

    def zg_copy(r):
        rows = pl.ds(r * (L // GC), L // GC)
        return remote(g_ref.at[rows], COT.at[hd, rows], zg_s.at[r], zg_r.at[r], (t, far))

    def zg_wait(r):
        rows = pl.ds(r * (L // GC), L // GC)
        remote(COT.at[far, rows], COT.at[far, rows], zg_s.at[r], zg_r.at[r], (t, far)).wait_recv()

    def cf_copy(r):
        rows = pl.ds(r * (L // GC), L // GC)
        return remote(COT.at[far, rows], COT.at[far, rows], cf_s.at[r], cf_r.at[r], (t, mate))

    def cf_wait(r):
        rows = pl.ds(r * (L // GC), L // GC)
        remote(
            COT.at[far_mate, rows], COT.at[far_mate, rows], cf_s.at[r], cf_r.at[r], (t, mate)
        ).wait_recv()

    co_copy = remote(g_ref, COT.at[hd], co_s, co_r, (t, mate))
    co_arrival = remote(COT.at[mate], COT.at[mate], co_s, co_r, (t, mate))

    def send_kv(h, first):
        for n in range(2):
            copies = kv_copies(n, h)
            for condition, copy in copies[:-1] if first else copies[-1:]:
                when(condition, copy.start)

    co_copy.start()
    for r in range(EARLY_ZG):
        zg_copy(r).start()

    def piece(buf, i):
        i = i % NP
        return buf.at[i // 8, :, pl.ds(pl.multiple_of((i % 8) * 32, 32), 32), :]

    for n in range(3 * H):
        load_own(n).wait()

    @pl.when(t == 0)
    def _():
        for h in range(H):
            second = sink_ref[h].astype(F32)
            for n in range(2):
                a = KV[n, h, pl.ds(L, T)].astype(F32)
                b = KV[n, h, pl.ds(L + T, T)].astype(F32)
                RB[n, h] = (a * (1.0 - second) + b * second).astype(BF)
        SB[0, :, pl.ds(0, 32), :] = RB[0, :, pl.ds(0, 32), :]

        def scatter(i, _):
            remote(piece(RB, i), piece(SB, i), sc_s.at[i], sc_r, (i, hd)).start()
            return 0

        lax.fori_loop(1, NP, scatter, 0)

    @pl.when(t != 0)
    def _():
        remote(piece(SB, t), piece(SB, t), sc_s.at[1], sc_r, (0, hd)).wait_recv()

    over = remote(piece(SB, t), piece(SB, t), sc_s.at[0], sc_r, ((t + NP) % NT, hd))
    when(zl == 0, over.start)

    def ag_copy(i):
        to = zl * NP + (t + i) % NP
        return remote(piece(SB, t), piece(SB, t), ag_s.at[i], ag_r.at[t % NP], (to, hd))

    def ag_start(i, _):
        ag_copy(i).start()
        return 0

    lax.fori_loop(1, NP, ag_start, 0)
    for r in range(EARLY_ZG, GC):
        zg_copy(r).start()
    for h in (3, 4, 1, 2):
        send_kv(h, True)
    for h in range(H):
        send_kv(h, False)

    def use_rows(s, r, first=False):
        rows = pl.ds(pl.multiple_of(r * (L // GC), L // GC), L // GC)
        for half in range(2):
            turned = COT[s, rows, pl.ds(half * YB, YB)].T
            for i in range(4):
                COTT[2 * s + half, i, :, rows] = turned[i * XB : (i + 1) * XB]
        got = mmt(COT[s, rows], W[s])
        GA[rows] = got if first else GA[rows] + got

    def use_block(s, first):
        def body(r, _):
            use_rows(s, r, first)
            return 0

        lax.fori_loop(0, GC, body, 0)

    load_g.wait()
    for s in range(4):
        load_w(s).wait()
    use_block(hd, True)
    co_arrival.wait_recv()
    use_block(mate, False)

    def ag_wait(i, _):
        src = zl * NP + (t + i) % NP
        remote(piece(SB, src), piece(SB, src), ag_s.at[i], ag_r.at[src % NP], (src, hd)).wait_recv()
        return 0

    lax.fori_loop(1, NP, ag_wait, 0)

    @pl.when(t == 0)
    def _():
        KV[:, :, pl.ds(0, L)] = jnp.zeros((2, H, L, HD), BF)

    def biases(h, i):
        f = 2 * t + i
        win, snk = win_ref[h], sink_ref[h]
        off = jnp.float32(-1e30)
        on = jnp.float32(0.0)
        return (
            jnp.where((win >= 3) & (f >= 2), on, off),
            jnp.where((win >= 2) & (f >= 1), on, off),
            None,
            jnp.where(snk <= f - win, on, off),
        )

    def forward(h):
        vt = KV[1, h].T
        svt = SB[1, h].T
        for i in range(2):
            q = Q[h, pl.ds(i * T, T)]
            peak = None
            scores = []
            for b, bias in enumerate(biases(h, i)):
                keys = KV[0, h, pl.ds((i + b) * T, T)] if b < 3 else SB[0, h]
                s = mmt(keys, q) * SCALE2
                if bias is not None:
                    s = s + bias
                top = jnp.max(s, axis=0, keepdims=True)
                peak = top if peak is None else jnp.maximum(peak, top)
                scores.append(s)
            weights = [jnp.exp2(s - peak) for s in scores]
            total = sum(jnp.sum(e, axis=0, keepdims=True) for e in weights)
            inverse = 1.0 / total
            out = None
            for b, e in enumerate(weights):
                p = e * inverse
                PR[2 * h + i, pl.ds(b * T, T)] = p
                values = vt[:, (i + b) * T : (i + b + 1) * T] if b < 3 else svt
                term = mm(values, p.astype(BF))
                out = term if out is None else out + term
            ATT[h, :, pl.ds(i * T, T)] = out.astype(BF)

    row_start = (x == 0) & (y > 0)
    row_relay_back = (x == 0) & (y < 3)

    def d_direct(h):
        return remote(DPS.at[h], DPR.at[h], d_s.at[h], d_r.at[h], ((t + NT - 1) % NT, hd))

    def d_first(h):
        return remote(DPS.at[h], RLD.at[h - 3], d_s.at[h], rd_r.at[h - 3], ((t + NT - 4) % NT, hd))

    def d_onward(h):
        return remote(RLD.at[h - 3], DPR.at[h], rd_s.at[h - 3], d_r.at[h], ((t + 3) % NT, hd))

    def out_copy(n, h):
        ref = (dq_ref, dk_ref, dv_ref)[n]
        src = DQ.at[h] if n == 0 else DKV.at[n - 1, h]
        return pltpu.make_async_copy(src, ref.at[:, pl.ds(pl.multiple_of(h * HD, HD), HD)], o_sem.at[n, h])

    def backward(h):
        kt = KV[0, h].T
        skt = SB[0, h].T
        near = []
        for i in range(2):
            q = Q[h, pl.ds(i * T, T)]
            do = GA[pl.ds(i * T, T), pl.ds(pl.multiple_of(h * HD, HD), HD)].astype(BF)
            grads = []
            delta = None
            for b in range(4):
                values = KV[1, h, pl.ds((i + b) * T, T)] if b < 3 else SB[1, h]
                dp = mmt(values, do)
                term = jnp.sum(PR[2 * h + i, pl.ds(b * T, T)] * dp, axis=0, keepdims=True)
                delta = term if delta is None else delta + term
                grads.append(dp)
            out = None
            terms = []
            for b in range(4):
                p = PR[2 * h + i, pl.ds(b * T, T)]
                ds = (p * (grads[b] - delta) * SCALE).astype(BF)
                keys = kt[:, (i + b) * T : (i + b + 1) * T] if b < 3 else skt
                term = mm(keys, ds)
                out = term if out is None else out + term
                if b < 3:
                    terms.append((mm(ds, q), mm(p.astype(BF), do)))
            DQ[h, pl.ds(i * T, T)] = out.T.astype(BF)
            near.append(terms)
        out_copy(0, h).start()
        for n in range(2):
            DPS[h, n, pl.ds(0, T)] = near[0][0][n].astype(BF)
            DPS[h, n, pl.ds(T, T)] = (near[0][1][n] + near[1][0][n]).astype(BF)
            PR[2 * h, pl.ds(0, T), pl.ds(n * HD, HD)] = near[0][2][n] + near[1][1][n]
            PR[2 * h, pl.ds(T, T), pl.ds(n * HD, HD)] = near[1][2][n]
        when((t > 0) & jnp.logical_not(row_start & (h >= 3)), lambda: d_direct(h).start())
        when(row_start & (h >= 3), lambda: d_first(h).start())

    def finish_kv(h):
        @pl.when(t < NT - 1)
        def _():
            d_direct(h).wait_recv()

        @pl.when(t == NT - 1)
        def _():
            DPR[h] = jnp.zeros((2, L, HD), BF)

        for n in range(2):
            own = PR[2 * h, pl.ds(0, L), pl.ds(n * HD, HD)]
            DKV[n, h] = (own + DPR[h, n].astype(F32)).astype(BF)
            out_copy(n + 1, h).start()

    def which(j):
        h = j % H
        turned = (j >= H) & ((h == X_FIRST[0]) | (h == X_FIRST[1]))
        return (zh + j // H) % 2, h, turned, jnp.where(turned, x, y), jnp.where(turned, y, x)

    def way(j):
        return jnp.where((j < H) & (j != EARLY_PLUS), -1, 1)

    def part(j, at):
        g, h, turned, _, _ = which(j)
        rows = jnp.concatenate(
            [COTT[g * 4 + jnp.where(turned, i, at), jnp.where(turned, at, i)] for i in range(4)]
        )
        return mmt(rows, ATT[h])

    def y_copy(j, m):
        _, _, turned, y1, _ = which(j)
        to = (y1 + (way(j) if m != 1 else -way(j)) + 4) % 4
        dev = zl * 16 + jnp.where(turned, y * 4 + to, to * 4 + x)
        return remote(YS.at[j, m], YR.at[j, m], y_s.at[j, m], y_r.at[j, m], (dev, hd))

    def x_copy(j, m):
        _, _, turned, _, x1 = which(j)
        to = (x1 + (way(j) if m != 1 else -way(j)) + 4) % 4
        dev = zl * 16 + jnp.where(turned, to * 4 + x, y * 4 + to)
        return remote(XS.at[j, m], XR.at[j, m], x_s.at[j, m], x_r.at[j, m], (dev, hd))

    def z_copy(h):
        return remote(ZS.at[h], ZR.at[h], z_s.at[h], z_r.at[h], ((t + 16) % NT, hd))

    def step1(j):
        y1 = which(j)[3]
        YS[j, 0] = part(j, (y1 + 2) % 4).astype(BF)
        y_copy(j, 0).start()
        YS[j, 1] = part(j, (y1 - way(j) + 4) % 4).astype(BF)
        y_copy(j, 1).start()

    def step2(j):
        own = part(j, (which(j)[3] + way(j) + 4) % 4)
        y_copy(j, 0).wait_recv()
        YS[j, 2] = (own + YR[j, 0].astype(F32)).astype(BF)
        y_copy(j, 2).start()

    def x_rows(xx):
        return pl.ds(pl.multiple_of(xx * XB, XB), XB)

    def step3(j):
        _, _, _, y1, x1 = which(j)
        own = part(j, y1)
        y_copy(j, 1).wait_recv()
        y_copy(j, 2).wait_recv()
        YSUM[...] = own + YR[j, 1].astype(F32) + YR[j, 2].astype(F32)
        XS[j, 0] = YSUM[x_rows((x1 + 2) % 4)].astype(BF)
        x_copy(j, 0).start()
        XS[j, 1] = YSUM[x_rows((x1 - way(j) + 4) % 4)].astype(BF)
        x_copy(j, 1).start()
        XK[j, 0] = YSUM[x_rows((x1 + way(j) + 4) % 4)]
        XK[j, 1] = YSUM[x_rows(x1)]

    def step4(j):
        x_copy(j, 0).wait_recv()
        XS[j, 2] = (XK[j, 0] + XR[j, 0].astype(F32)).astype(BF)
        x_copy(j, 2).start()

    def step5(j):
        g, h, _, _, _ = which(j)
        x_copy(j, 1).wait_recv()
        x_copy(j, 2).wait_recv()
        ZF[g, h] = XK[j, 1] + XR[j, 1].astype(F32) + XR[j, 2].astype(F32)

        @pl.when(j >= H)
        def _():
            ZS[h] = ZF[1 - zl, h].astype(BF)
            z_copy(h).start()

    def step6(h):
        z_copy(h).wait_recv()
        at = pl.ds(pl.multiple_of(h * HD, HD), HD)
        WO[at] = (ZF[zl, h] + ZR[h].astype(F32)).T

    def turn(j, _):
        for at, mine, onward, arrival in kv_relays():
            when(mine & (j == at), arrival.wait_recv)
            when(mine & (j == at), onward.start)

        @pl.when((j >= 2) & (j < GC + 2))
        def _():
            cf_wait(j - 2)
            use_rows(far_mate, j - 2)

        @pl.when(j < H)
        def _():
            @pl.when(t > 0)
            def _():
                for n in range(2):
                    place = KV.at[n, j, pl.ds(0, L)]
                    remote(place, place, kv_s.at[n, j], kv_r.at[n, j], ((t + 1) % NT, hd)).wait_recv()

            forward(j)

        @pl.when((j >= H) & (j < 2 * H))
        def _():
            backward(j - H)

        @pl.when(j < 2 * H)
        def _():
            step1(j)

        @pl.when((j >= 1) & (j < 2 * H + 1))
        def _():
            step2(j - 1)

        @pl.when((j >= 1) & (j < GC + 1))
        def _():
            zg_wait(j - 1)
            cf_copy(j - 1).start()
            use_rows(far, j - 1)

        @pl.when((j >= 2) & (j < 2 * H + 2))
        def _():
            step3(j - 2)

        @pl.when((j >= 3) & (j < 2 * H + 3))
        def _():
            step4(j - 3)

        @pl.when(row_relay_back & (j >= 2 * H) & (j < 2 * H + 2))
        def _():
            h = j - 2 * H + 3
            remote(RLD.at[h - 3], RLD.at[h - 3], rd_s.at[h - 3], rd_r.at[h - 3], (t, hd)).wait_recv()
            d_onward(h).start()

        @pl.when((j >= H + 3) & (j < 2 * H + 3))
        def _():
            finish_kv(j - H - 3)

        @pl.when((j >= 4) & (j < 2 * H + 4))
        def _():
            step5(j - 4)

        @pl.when(j >= H + 5)
        def _():
            step6(j - H - 5)

        return 0

    lax.fori_loop(0, 2 * H + 5, turn, 0)
    put_w = pltpu.make_async_copy(WO, wo_ref, w_sem.at[4])
    put_w.start()

    when(zl == 0, over.wait_send)
    co_copy.wait_send()
    for r in range(GC):
        zg_copy(r).wait_send()
        cf_copy(r).wait_send()

    @pl.when(t == 0)
    def _():
        def sent(i, _):
            remote(piece(RB, i), piece(SB, i), sc_s.at[i], sc_r, (i, hd)).wait_send()
            return 0

        lax.fori_loop(1, NP, sent, 0)

    def ag_sent(i, _):
        ag_copy(i).wait_send()
        return 0

    lax.fori_loop(1, NP, ag_sent, 0)

    def rs_sent(j, _):
        for m in range(3):
            y_copy(j, m).wait_send()
            x_copy(j, m).wait_send()
        return 0

    lax.fori_loop(0, 2 * H, rs_sent, 0)
    for h in range(H):
        for n in range(2):
            for condition, copy in kv_copies(n, h):
                when(condition, copy.wait_send)
        z_copy(h).wait_send()
        when(t > 0, d_direct(h).wait_send)
        for n in range(3):
            out_copy(n, h).wait()
    for _, mine, onward, _ in kv_relays():
        when(mine, onward.wait_send)
    for h in (3, 4):
        when(row_relay_back, d_onward(h).wait_send)
    put_w.wait()


def hand_over(a, b, c, d, a_out, b_out, c_out, d_out, a_mid, b_mid, c_mid, d_mid, sem):
    arrays = ((a, a_mid, a_out), (b, b_mid, b_out), (c, c_mid, c_out), (d, d_mid, d_out))
    copies = [
        (pltpu.make_async_copy(src, mid, sem.at[0, i]), pltpu.make_async_copy(mid, dst, sem.at[1, i]))
        for i, (src, mid, dst) in enumerate(arrays)
    ]
    for load, _ in copies:
        load.start()
    for load, store in copies:
        load.wait()
        store.start()
    for _, store in copies:
        store.wait()


def per_device(query, key, value, out_weight, grad_out, sink_frame, window):
    dma = pltpu.SemaphoreType.DMA
    any_spec = pl.BlockSpec(memory_space=pl.ANY)
    smem = pl.BlockSpec(memory_space=pltpu.SMEM)
    sds = jax.ShapeDtypeStruct
    grad_query, grad_key, grad_value, weight = pl.pallas_call(
        kernel,
        out_shape=[sds((L, H * HD), BF)] * 3 + [sds((H * HD, XB), F32)],
        in_specs=[any_spec] * 5 + [smem] * 2,
        out_specs=[any_spec] * 4,
        scratch_shapes=[
            pltpu.VMEM((H, L, HD), BF),
            pltpu.VMEM((2, H, 2 * L, HD), BF),
            pltpu.VMEM((2, H, T, HD), BF),
            pltpu.VMEM((2, H, T, HD), BF),
            pltpu.VMEM((2, 2, L, HD), BF),
            pltpu.VMEM((2, 2, L, HD), BF),
            pltpu.VMEM((4, L, CW), BF),
            pltpu.VMEM((8, 4, XB, L), BF),
            pltpu.VMEM((4, H * HD, CW), BF),
            pltpu.VMEM((L, H * HD), F32),
            pltpu.VMEM((2 * H, 4 * T, T), F32),
            pltpu.VMEM((H, HD, L), BF),
            pltpu.VMEM((2 * H, 3, YB, HD), BF),
            pltpu.VMEM((2 * H, 3, YB, HD), BF),
            pltpu.VMEM((YB, HD), F32),
            pltpu.VMEM((2 * H, 3, XB, HD), BF),
            pltpu.VMEM((2 * H, 3, XB, HD), BF),
            pltpu.VMEM((2 * H, 2, XB, HD), F32),
            pltpu.VMEM((2, H, XB, HD), F32),
            pltpu.VMEM((H, XB, HD), BF),
            pltpu.VMEM((H, XB, HD), BF),
            pltpu.VMEM((H * HD, XB), F32),
            pltpu.VMEM((H, 2, L, HD), BF),
            pltpu.VMEM((H, 2, L, HD), BF),
            pltpu.VMEM((H, L, HD), BF),
            pltpu.VMEM((2, H, L, HD), BF),
            dma((3 * H,)), dma((5,)),
            dma((2, H)), dma((2, H)), dma((2, 2)), dma((2, 2)), dma((2,)), dma((2,)),
            dma((GC,)), dma((GC,)),
            dma, dma,
            dma((GC,)), dma((GC,)),
            dma((NT,)), dma,
            dma((NP,)), dma((NP,)),
            dma((2 * H, 3)), dma((2 * H, 3)),
            dma((2 * H, 3)), dma((2 * H, 3)),
            dma((H,)), dma((H,)),
            dma((H,)), dma((H,)),
            dma((3, H)),
        ],
        compiler_params=pltpu.CompilerParams(
            collective_id=0, has_side_effects=True, vmem_limit_bytes=60 * 1024 * 1024
        ),
        name="layer_backward",
    )(query, key, value, out_weight, grad_out, sink_frame, window)
    outs = [sds((L, H * HD), BF)] * 3 + [sds((H * HD, XB), F32)]
    return tuple(
        pl.pallas_call(
            hand_over,
            out_shape=outs,
            in_specs=[any_spec] * 4,
            out_specs=[any_spec] * 4,
            scratch_shapes=[pltpu.VMEM(o.shape, o.dtype) for o in outs] + [dma((2, 4))],
            compiler_params=pltpu.CompilerParams(vmem_limit_bytes=60 * 1024 * 1024),
            name="hand_over",
        )(grad_query, grad_key, grad_value, weight)
    )


def solution(mesh):
    placed = (
        P("tm", "head"),
        P("tm", "head"),
        P("tm", "head"),
        P("head", None),
        P("tm", "head"),
        P("head"),
        P("head"),
    )
    return jax.shard_map(
        per_device,
        mesh=mesh,
        in_specs=placed,
        out_specs=(P("tm", "head"), P("tm", "head"), P("tm", "head"), P("head", "tm")),
        check_vma=False,
    )
```

```python
import math

import jax
import jax.numpy as jnp
from jax import lax
from jax.experimental import pallas as pl
from jax.experimental.pallas import tpu as pltpu
from jax.sharding import PartitionSpec as P

MESH = pl.DeviceIdType.MESH
BF = jnp.bfloat16
F32 = jnp.float32
NP = 16
NT = 32
H = 5
HD = 128
T = 256
L = 2 * T
SCALE = 1.0 / math.sqrt(HD)
SCALE2 = SCALE * math.log2(math.e)
CW = 1280
GC = 4
YB = 640
XB = 160
LAST = ((1,), (1,))
EARLY_ZG = 0
Z_RELAY = {1: 17, 2: 20, 3: 28, 4: 19}
X_FIRST = (1, 3)
LAG2, LAG3, LAG4, LAG5, LAG6 = 1, 2, 3, 4, 5


def mm(a, b):
    return lax.dot_general(a, b, (((1,), (0,)), ((), ())), preferred_element_type=F32)


def mmt(a, b):
    return lax.dot_general(a, b, (LAST, ((), ())), preferred_element_type=F32)


def kernel(
    q_ref, k_ref, v_ref, w_ref, g_ref, sink_ref, win_ref,
    dq_ref, dk_ref, dv_ref, wo_ref,
    Q, KV, SB, RB, RL, RLD, COT, COTT, W, GA, PR, ATT, YS, YR, YSUM, XS, XR, XK, ZF, ZS, ZR, WO,
    DPS, DPR, DQ, DKV,
    l_sem, w_sem, kv_s, kv_r, rl_r, rl_s, rd_r, rd_s, zg_s, zg_r, co_s, co_r, cf_s, cf_r, sc_s, sc_r, ag_s, ag_r,
    y_s, y_r, x_s, x_r, z_s, z_r, d_s, d_r, o_sem,
):
    t = lax.axis_index("tm")
    hd = lax.axis_index("head")
    zl, y, x = t // 16, (t // 4) % 4, t % 4
    zh, core = hd // 2, hd % 2
    mate = hd + 1 - 2 * core
    far = (hd + 2) % 4
    far_mate = (mate + 2) % 4

    def remote(src, dst, ss, rs, dev):
        return pltpu.make_async_remote_copy(
            src_ref=src, dst_ref=dst, send_sem=ss, recv_sem=rs, device_id=dev, device_id_type=MESH
        )

    def load_own(n):
        ref = (k_ref, v_ref)[n // H] if n < 2 * H else q_ref
        h = n % H
        dst = KV.at[n // H, h, pl.ds(L, L)] if n < 2 * H else Q.at[h]
        return pltpu.make_async_copy(ref.at[:, pl.ds(h * HD, HD)], dst, l_sem.at[n])

    def load_w(s):
        return pltpu.make_async_copy(w_ref.at[:, pl.ds(s * CW, CW)], W.at[s], w_sem.at[s])

    load_g = pltpu.make_async_copy(g_ref, COT.at[hd], w_sem.at[4])
    for n in range(3 * H):
        load_own(n).start()
    load_g.start()
    for s in range(4):
        load_w(s).start()

    barrier = pltpu.get_barrier_semaphore()

    def greet(i, _):
        pl.semaphore_signal(barrier, inc=1, device_id=((t + i) % NT, hd), device_id_type=MESH)
        return 0

    lax.fori_loop(1, NT, greet, 0)
    pl.semaphore_signal(barrier, inc=1, device_id=(t, mate), device_id_type=MESH)
    pl.semaphore_signal(barrier, inc=1, device_id=(t, far), device_id_type=MESH)
    pl.semaphore_wait(barrier, NT + 1)

    row_end = (x == 3) & (y < 3)
    plane_end = t == NT // 2 - 1
    row_relay = (x == 3) & (y > 0)

    def kv_copies(n, h):
        src = (k_ref, v_ref)[n].at[:, pl.ds(h * HD, HD)]
        sem = kv_s.at[n, h]
        out = []
        direct = t < NT - 1
        if h >= 3:
            out.append((row_end, remote(src, RL.at[h - 3, n], sem, rl_r.at[h - 3, n], (t + 4, hd))))
            direct = direct & jnp.logical_not(row_end)
        if h in Z_RELAY:
            to = Z_RELAY[h]
            out.append((plane_end, remote(src, RL.at[0, n], sem, rl_r.at[0, n], (to, hd))))
            direct = direct & jnp.logical_not(plane_end)
        place = KV.at[n, h, pl.ds(0, L)]
        out.append((direct, remote(src, place, sem, kv_r.at[n, h], ((t + 1) % NT, hd))))
        return out

    def kv_relays():
        roles = [(row_relay, 0, 3, (t + NT - 3) % NT, 1), (row_relay, 1, 4, (t + NT - 3) % NT, 2)]
        roles += [(t == at, 0, h, NT // 2, h - 1) for h, at in Z_RELAY.items()]
        for mine, slot, h, to, turn in roles:
            for n in range(2):
                yield turn, mine, remote(
                    RL.at[slot, n], KV.at[n, h, pl.ds(0, L)], rl_s.at[slot, n], kv_r.at[n, h], (to, hd)
                ), remote(RL.at[slot, n], RL.at[slot, n], rl_s.at[slot, n], rl_r.at[slot, n], (to, hd))

    def when(condition, act):
        @pl.when(condition)
        def _():
            act()

    def zg_copy(r):
        rows = pl.ds(r * (L // GC), L // GC)
        return remote(g_ref.at[rows], COT.at[hd, rows], zg_s.at[r], zg_r.at[r], (t, far))

    def zg_wait(r):
        rows = pl.ds(r * (L // GC), L // GC)
        remote(COT.at[far, rows], COT.at[far, rows], zg_s.at[r], zg_r.at[r], (t, far)).wait_recv()

    def cf_copy(r):
        rows = pl.ds(r * (L // GC), L // GC)
        return remote(COT.at[far, rows], COT.at[far, rows], cf_s.at[r], cf_r.at[r], (t, mate))

    def cf_wait(r):
        rows = pl.ds(r * (L // GC), L // GC)
        remote(
            COT.at[far_mate, rows], COT.at[far_mate, rows], cf_s.at[r], cf_r.at[r], (t, mate)
        ).wait_recv()

    co_copy = remote(g_ref, COT.at[hd], co_s, co_r, (t, mate))
    co_arrival = remote(COT.at[mate], COT.at[mate], co_s, co_r, (t, mate))

    def send_kv(h, first):
        for n in range(2):
            copies = kv_copies(n, h)
            for condition, copy in copies[:-1] if first else copies[-1:]:
                when(condition, copy.start)

    co_copy.start()
    for r in range(EARLY_ZG):
        zg_copy(r).start()

    def piece(buf, i):
        i = i % NP
        return buf.at[i // 8, :, pl.ds(pl.multiple_of((i % 8) * 32, 32), 32), :]

    for n in range(3 * H):
        load_own(n).wait()

    @pl.when(t == 0)
    def _():
        for h in range(H):
            second = sink_ref[h].astype(F32)
            for n in range(2):
                a = KV[n, h, pl.ds(L, T)].astype(F32)
                b = KV[n, h, pl.ds(L + T, T)].astype(F32)
                RB[n, h] = (a * (1.0 - second) + b * second).astype(BF)
        SB[0, :, pl.ds(0, 32), :] = RB[0, :, pl.ds(0, 32), :]

        def scatter(i, _):
            remote(piece(RB, i), piece(SB, i), sc_s.at[i], sc_r, (i, hd)).start()
            return 0

        lax.fori_loop(1, NP, scatter, 0)

    @pl.when(t != 0)
    def _():
        remote(piece(SB, t), piece(SB, t), sc_s.at[1], sc_r, (0, hd)).wait_recv()

    over = remote(piece(SB, t), piece(SB, t), sc_s.at[0], sc_r, ((t + NP) % NT, hd))
    when(zl == 0, over.start)

    def ag_copy(i):
        to = zl * NP + (t + i) % NP
        return remote(piece(SB, t), piece(SB, t), ag_s.at[i], ag_r.at[t % NP], (to, hd))

    def ag_start(i, _):
        ag_copy(i).start()
        return 0

    lax.fori_loop(1, NP, ag_start, 0)
    for r in range(EARLY_ZG, GC):
        zg_copy(r).start()
    for h in (3, 4, 1, 2):
        send_kv(h, True)
    for h in range(H):
        send_kv(h, False)

    def use_rows(s, r, first=False):
        rows = pl.ds(pl.multiple_of(r * (L // GC), L // GC), L // GC)
        for half in range(2):
            turned = COT[s, rows, pl.ds(half * YB, YB)].T
            for i in range(4):
                COTT[2 * s + half, i, :, rows] = turned[i * XB : (i + 1) * XB]
        got = mmt(COT[s, rows], W[s])
        GA[rows] = got if first else GA[rows] + got

    def use_block(s, first):
        def body(r, _):
            use_rows(s, r, first)
            return 0

        lax.fori_loop(0, GC, body, 0)

    load_g.wait()
    for s in range(4):
        load_w(s).wait()
    use_block(hd, True)
    co_arrival.wait_recv()
    use_block(mate, False)

    def ag_wait(i, _):
        src = zl * NP + (t + i) % NP
        remote(piece(SB, src), piece(SB, src), ag_s.at[i], ag_r.at[src % NP], (src, hd)).wait_recv()
        return 0

    lax.fori_loop(1, NP, ag_wait, 0)

    @pl.when(t == 0)
    def _():
        KV[:, :, pl.ds(0, L)] = jnp.zeros((2, H, L, HD), BF)

    def biases(h, i):
        f = 2 * t + i
        win, snk = win_ref[h], sink_ref[h]
        off = jnp.float32(-1e30)
        on = jnp.float32(0.0)
        return (
            jnp.where((win >= 3) & (f >= 2), on, off),
            jnp.where((win >= 2) & (f >= 1), on, off),
            None,
            jnp.where(snk <= f - win, on, off),
        )

    def forward(h):
        vt = KV[1, h].T
        svt = SB[1, h].T
        for i in range(2):
            q = Q[h, pl.ds(i * T, T)]
            peak = None
            scores = []
            for b, bias in enumerate(biases(h, i)):
                keys = KV[0, h, pl.ds((i + b) * T, T)] if b < 3 else SB[0, h]
                s = mmt(keys, q) * SCALE2
                if bias is not None:
                    s = s + bias
                top = jnp.max(s, axis=0, keepdims=True)
                peak = top if peak is None else jnp.maximum(peak, top)
                scores.append(s)
            weights = [jnp.exp2(s - peak) for s in scores]
            total = sum(jnp.sum(e, axis=0, keepdims=True) for e in weights)
            inverse = 1.0 / total
            out = None
            for b, e in enumerate(weights):
                p = e * inverse
                PR[2 * h + i, pl.ds(b * T, T)] = p
                values = vt[:, (i + b) * T : (i + b + 1) * T] if b < 3 else svt
                term = mm(values, p.astype(BF))
                out = term if out is None else out + term
            ATT[h, :, pl.ds(i * T, T)] = out.astype(BF)

    row_start = (x == 0) & (y > 0)
    row_relay_back = (x == 0) & (y < 3)

    def d_direct(h):
        return remote(DPS.at[h], DPR.at[h], d_s.at[h], d_r.at[h], ((t + NT - 1) % NT, hd))

    def d_first(h):
        return remote(DPS.at[h], RLD.at[h - 3], d_s.at[h], rd_r.at[h - 3], ((t + NT - 4) % NT, hd))

    def d_onward(h):
        return remote(RLD.at[h - 3], DPR.at[h], rd_s.at[h - 3], d_r.at[h], ((t + 3) % NT, hd))

    def out_copy(n, h):
        ref = (dq_ref, dk_ref, dv_ref)[n]
        src = DQ.at[h] if n == 0 else DKV.at[n - 1, h]
        return pltpu.make_async_copy(src, ref.at[:, pl.ds(pl.multiple_of(h * HD, HD), HD)], o_sem.at[n, h])

    def backward(h):
        kt = KV[0, h].T
        skt = SB[0, h].T
        near = []
        for i in range(2):
            q = Q[h, pl.ds(i * T, T)]
            do = GA[pl.ds(i * T, T), pl.ds(pl.multiple_of(h * HD, HD), HD)].astype(BF)
            grads = []
            delta = None
            for b in range(4):
                values = KV[1, h, pl.ds((i + b) * T, T)] if b < 3 else SB[1, h]
                dp = mmt(values, do)
                term = jnp.sum(PR[2 * h + i, pl.ds(b * T, T)] * dp, axis=0, keepdims=True)
                delta = term if delta is None else delta + term
                grads.append(dp)
            out = None
            terms = []
            for b in range(4):
                p = PR[2 * h + i, pl.ds(b * T, T)]
                ds = (p * (grads[b] - delta) * SCALE).astype(BF)
                keys = kt[:, (i + b) * T : (i + b + 1) * T] if b < 3 else skt
                term = mm(keys, ds)
                out = term if out is None else out + term
                if b < 3:
                    terms.append((mm(ds, q), mm(p.astype(BF), do)))
            DQ[h, pl.ds(i * T, T)] = out.T.astype(BF)
            near.append(terms)
        out_copy(0, h).start()
        for n in range(2):
            DPS[h, n, pl.ds(0, T)] = near[0][0][n].astype(BF)
            DPS[h, n, pl.ds(T, T)] = (near[0][1][n] + near[1][0][n]).astype(BF)
            PR[2 * h, pl.ds(0, T), pl.ds(n * HD, HD)] = near[0][2][n] + near[1][1][n]
            PR[2 * h, pl.ds(T, T), pl.ds(n * HD, HD)] = near[1][2][n]
        when((t > 0) & jnp.logical_not(row_start & (h >= 3)), lambda: d_direct(h).start())
        when(row_start & (h >= 3), lambda: d_first(h).start())

    def finish_kv(h):
        @pl.when(t < NT - 1)
        def _():
            d_direct(h).wait_recv()

        @pl.when(t == NT - 1)
        def _():
            DPR[h] = jnp.zeros((2, L, HD), BF)

        for n in range(2):
            own = PR[2 * h, pl.ds(0, L), pl.ds(n * HD, HD)]
            DKV[n, h] = (own + DPR[h, n].astype(F32)).astype(BF)
            out_copy(n + 1, h).start()

    def which(j):
        h = j % H
        turned = (j >= H) & ((h == X_FIRST[0]) | (h == X_FIRST[1]))
        return (zh + j // H) % 2, h, turned, jnp.where(turned, x, y), jnp.where(turned, y, x)

    def way(j):
        return jnp.where((j < H) & (j != 3), -1, 1)

    def part(j, at):
        g, h, turned, _, _ = which(j)
        rows = jnp.concatenate(
            [COTT[g * 4 + jnp.where(turned, i, at), jnp.where(turned, at, i)] for i in range(4)]
        )
        return mmt(rows, ATT[h])

    def y_copy(j, m):
        _, _, turned, y1, _ = which(j)
        to = (y1 + (way(j) if m != 1 else -way(j)) + 4) % 4
        dev = zl * 16 + jnp.where(turned, y * 4 + to, to * 4 + x)
        return remote(YS.at[j, m], YR.at[j, m], y_s.at[j, m], y_r.at[j, m], (dev, hd))

    def x_copy(j, m):
        _, _, turned, _, x1 = which(j)
        to = (x1 + (way(j) if m != 1 else -way(j)) + 4) % 4
        dev = zl * 16 + jnp.where(turned, to * 4 + x, y * 4 + to)
        return remote(XS.at[j, m], XR.at[j, m], x_s.at[j, m], x_r.at[j, m], (dev, hd))

    def z_copy(h):
        return remote(ZS.at[h], ZR.at[h], z_s.at[h], z_r.at[h], ((t + 16) % NT, hd))

    def step1(j):
        y1 = which(j)[3]
        YS[j, 0] = part(j, (y1 + 2) % 4).astype(BF)
        y_copy(j, 0).start()
        YS[j, 1] = part(j, (y1 - way(j) + 4) % 4).astype(BF)
        y_copy(j, 1).start()

    def step2(j):
        own = part(j, (which(j)[3] + way(j) + 4) % 4)
        y_copy(j, 0).wait_recv()
        YS[j, 2] = (own + YR[j, 0].astype(F32)).astype(BF)
        y_copy(j, 2).start()

    def x_rows(xx):
        return pl.ds(pl.multiple_of(xx * XB, XB), XB)

    def step3(j):
        _, _, _, y1, x1 = which(j)
        own = part(j, y1)
        y_copy(j, 1).wait_recv()
        y_copy(j, 2).wait_recv()
        YSUM[...] = own + YR[j, 1].astype(F32) + YR[j, 2].astype(F32)
        XS[j, 0] = YSUM[x_rows((x1 + 2) % 4)].astype(BF)
        x_copy(j, 0).start()
        XS[j, 1] = YSUM[x_rows((x1 - way(j) + 4) % 4)].astype(BF)
        x_copy(j, 1).start()
        XK[j, 0] = YSUM[x_rows((x1 + way(j) + 4) % 4)]
        XK[j, 1] = YSUM[x_rows(x1)]

    def step4(j):
        x_copy(j, 0).wait_recv()
        XS[j, 2] = (XK[j, 0] + XR[j, 0].astype(F32)).astype(BF)
        x_copy(j, 2).start()

    def step5(j):
        g, h, _, _, _ = which(j)
        x_copy(j, 1).wait_recv()
        x_copy(j, 2).wait_recv()
        ZF[g, h] = XK[j, 1] + XR[j, 1].astype(F32) + XR[j, 2].astype(F32)

        @pl.when(j >= H)
        def _():
            ZS[h] = ZF[1 - zl, h].astype(BF)
            z_copy(h).start()

    def step6(h):
        z_copy(h).wait_recv()
        at = pl.ds(pl.multiple_of(h * HD, HD), HD)
        WO[at] = (ZF[zl, h] + ZR[h].astype(F32)).T

    def turn(j, _):
        for at, mine, onward, arrival in kv_relays():
            when(mine & (j == at), arrival.wait_recv)
            when(mine & (j == at), onward.start)

        @pl.when((j >= 2) & (j < GC + 2))
        def _():
            cf_wait(j - 2)
            use_rows(far_mate, j - 2)

        @pl.when(j < H)
        def _():
            @pl.when(t > 0)
            def _():
                for n in range(2):
                    place = KV.at[n, j, pl.ds(0, L)]
                    remote(place, place, kv_s.at[n, j], kv_r.at[n, j], ((t + 1) % NT, hd)).wait_recv()

            forward(j)

        @pl.when(j < 2 * H)
        def _():
            step1(j)

        @pl.when((j >= LAG2) & (j < 2 * H + LAG2))
        def _():
            step2(j - LAG2)

        @pl.when((j >= 1) & (j < GC + 1))
        def _():
            zg_wait(j - 1)
            cf_copy(j - 1).start()
            use_rows(far, j - 1)

        @pl.when((j >= H) & (j < 2 * H))
        def _():
            backward(j - H)

        @pl.when((j >= LAG3) & (j < 2 * H + LAG3))
        def _():
            step3(j - LAG3)

        @pl.when((j >= LAG4) & (j < 2 * H + LAG4))
        def _():
            step4(j - LAG4)

        @pl.when(row_relay_back & (j >= 2 * H) & (j < 2 * H + 2))
        def _():
            h = j - 2 * H + 3
            remote(RLD.at[h - 3], RLD.at[h - 3], rd_s.at[h - 3], rd_r.at[h - 3], (t, hd)).wait_recv()
            d_onward(h).start()

        @pl.when((j >= H + 5) & (j < 2 * H + 5))
        def _():
            finish_kv(j - H - 5)

        @pl.when((j >= LAG5) & (j < 2 * H + LAG5))
        def _():
            step5(j - LAG5)

        @pl.when(j >= H + LAG6)
        def _():
            step6(j - H - LAG6)

        return 0

    lax.fori_loop(0, 2 * H + LAG6, turn, 0)
    put_w = pltpu.make_async_copy(WO, wo_ref, w_sem.at[4])
    put_w.start()

    when(zl == 0, over.wait_send)
    co_copy.wait_send()
    for r in range(GC):
        zg_copy(r).wait_send()
        cf_copy(r).wait_send()

    @pl.when(t == 0)
    def _():
        def sent(i, _):
            remote(piece(RB, i), piece(SB, i), sc_s.at[i], sc_r, (i, hd)).wait_send()
            return 0

        lax.fori_loop(1, NP, sent, 0)

    def ag_sent(i, _):
        ag_copy(i).wait_send()
        return 0

    lax.fori_loop(1, NP, ag_sent, 0)

    def rs_sent(j, _):
        for m in range(3):
            y_copy(j, m).wait_send()
            x_copy(j, m).wait_send()
        return 0

    lax.fori_loop(0, 2 * H, rs_sent, 0)
    for h in range(H):
        for n in range(2):
            for condition, copy in kv_copies(n, h):
                when(condition, copy.wait_send)
        z_copy(h).wait_send()
        when(t > 0, d_direct(h).wait_send)
        for n in range(3):
            out_copy(n, h).wait()
    for _, mine, onward, _ in kv_relays():
        when(mine, onward.wait_send)
    for h in (3, 4):
        when(row_relay_back, d_onward(h).wait_send)
    put_w.wait()


def hand_over(a, b, c, d, a_out, b_out, c_out, d_out, a_mid, b_mid, c_mid, d_mid, sem):
    arrays = ((a, a_mid, a_out), (b, b_mid, b_out), (c, c_mid, c_out), (d, d_mid, d_out))
    copies = [
        (pltpu.make_async_copy(src, mid, sem.at[0, i]), pltpu.make_async_copy(mid, dst, sem.at[1, i]))
        for i, (src, mid, dst) in enumerate(arrays)
    ]
    for load, _ in copies:
        load.start()
    for load, store in copies:
        load.wait()
        store.start()
    for _, store in copies:
        store.wait()


def per_device(query, key, value, out_weight, grad_out, sink_frame, window):
    dma = pltpu.SemaphoreType.DMA
    any_spec = pl.BlockSpec(memory_space=pl.ANY)
    smem = pl.BlockSpec(memory_space=pltpu.SMEM)
    sds = jax.ShapeDtypeStruct
    grad_query, grad_key, grad_value, weight = pl.pallas_call(
        kernel,
        out_shape=[sds((L, H * HD), BF)] * 3 + [sds((H * HD, XB), F32)],
        in_specs=[any_spec] * 5 + [smem] * 2,
        out_specs=[any_spec] * 4,
        scratch_shapes=[
            pltpu.VMEM((H, L, HD), BF),
            pltpu.VMEM((2, H, 2 * L, HD), BF),
            pltpu.VMEM((2, H, T, HD), BF),
            pltpu.VMEM((2, H, T, HD), BF),
            pltpu.VMEM((2, 2, L, HD), BF),
            pltpu.VMEM((2, 2, L, HD), BF),
            pltpu.VMEM((4, L, CW), BF),
            pltpu.VMEM((8, 4, XB, L), BF),
            pltpu.VMEM((4, H * HD, CW), BF),
            pltpu.VMEM((L, H * HD), F32),
            pltpu.VMEM((2 * H, 4 * T, T), F32),
            pltpu.VMEM((H, HD, L), BF),
            pltpu.VMEM((2 * H, 3, YB, HD), BF),
            pltpu.VMEM((2 * H, 3, YB, HD), BF),
            pltpu.VMEM((YB, HD), F32),
            pltpu.VMEM((2 * H, 3, XB, HD), BF),
            pltpu.VMEM((2 * H, 3, XB, HD), BF),
            pltpu.VMEM((2 * H, 2, XB, HD), F32),
            pltpu.VMEM((2, H, XB, HD), F32),
            pltpu.VMEM((H, XB, HD), BF),
            pltpu.VMEM((H, XB, HD), BF),
            pltpu.VMEM((H * HD, XB), F32),
            pltpu.VMEM((H, 2, L, HD), BF),
            pltpu.VMEM((H, 2, L, HD), BF),
            pltpu.VMEM((H, L, HD), BF),
            pltpu.VMEM((2, H, L, HD), BF),
            dma((3 * H,)), dma((5,)),
            dma((2, H)), dma((2, H)), dma((2, 2)), dma((2, 2)), dma((2,)), dma((2,)),
            dma((GC,)), dma((GC,)),
            dma, dma,
            dma((GC,)), dma((GC,)),
            dma((NT,)), dma,
            dma((NP,)), dma((NP,)),
            dma((2 * H, 3)), dma((2 * H, 3)),
            dma((2 * H, 3)), dma((2 * H, 3)),
            dma((H,)), dma((H,)),
            dma((H,)), dma((H,)),
            dma((3, H)),
        ],
        compiler_params=pltpu.CompilerParams(
            collective_id=0, has_side_effects=True, vmem_limit_bytes=60 * 1024 * 1024
        ),
        name="layer_backward",
    )(query, key, value, out_weight, grad_out, sink_frame, window)
    outs = [sds((L, H * HD), BF)] * 3 + [sds((H * HD, XB), F32)]
    return tuple(
        pl.pallas_call(
            hand_over,
            out_shape=outs,
            in_specs=[any_spec] * 4,
            out_specs=[any_spec] * 4,
            scratch_shapes=[pltpu.VMEM(o.shape, o.dtype) for o in outs] + [dma((2, 4))],
            compiler_params=pltpu.CompilerParams(vmem_limit_bytes=60 * 1024 * 1024),
            name="hand_over",
        )(grad_query, grad_key, grad_value, weight)
    )


def solution(mesh):
    placed = (
        P("tm", "head"),
        P("tm", "head"),
        P("tm", "head"),
        P("head", None),
        P("tm", "head"),
        P("head"),
        P("head"),
    )
    return jax.shard_map(
        per_device,
        mesh=mesh,
        in_specs=placed,
        out_specs=(P("tm", "head"), P("tm", "head"), P("tm", "head"), P("head", "tm")),
        check_vma=False,
    )
```

```python
import math

import jax
import jax.numpy as jnp
from jax import lax
from jax.experimental import pallas as pl
from jax.experimental.pallas import tpu as pltpu
from jax.sharding import PartitionSpec as P

MESH = pl.DeviceIdType.MESH
BF = jnp.bfloat16
F32 = jnp.float32
NP = 16
NT = 32
H = 5
HD = 128
T = 256
L = 2 * T
SCALE = 1.0 / math.sqrt(HD)
SCALE2 = SCALE * math.log2(math.e)
CW = 1280
GC = 4
YB = 640
XB = 160
LAST = ((1,), (1,))
EARLY_ZG = 0
Z_RELAY = {1: 17, 2: 20, 3: 28, 4: 19}
X_FIRST = (1, 3)
LAG2, LAG3, LAG4, LAG5, LAG6 = 1, 2, 3, 4, 5


def mm(a, b):
    return lax.dot_general(a, b, (((1,), (0,)), ((), ())), preferred_element_type=F32)


def mmt(a, b):
    return lax.dot_general(a, b, (LAST, ((), ())), preferred_element_type=F32)


def kernel(
    q_ref, k_ref, v_ref, w_ref, g_ref, sink_ref, win_ref,
    dq_ref, dk_ref, dv_ref, wo_ref,
    Q, KV, SB, RB, RL, RLD, COT, COTT, W, GA, PR, ATT, YS, YR, YSUM, XS, XR, XK, ZF, ZS, ZR, WO,
    DPS, DPR, DQ, DKV,
    l_sem, w_sem, kv_s, kv_r, rl_r, rl_s, rd_r, rd_s, zg_s, zg_r, co_s, co_r, cf_s, cf_r, sc_s, sc_r, ag_s, ag_r,
    y_s, y_r, x_s, x_r, z_s, z_r, d_s, d_r, o_sem,
):
    t = lax.axis_index("tm")
    hd = lax.axis_index("head")
    zl, y, x = t // 16, (t // 4) % 4, t % 4
    zh, core = hd // 2, hd % 2
    mate = hd + 1 - 2 * core
    far = (hd + 2) % 4
    far_mate = (mate + 2) % 4

    def remote(src, dst, ss, rs, dev):
        return pltpu.make_async_remote_copy(
            src_ref=src, dst_ref=dst, send_sem=ss, recv_sem=rs, device_id=dev, device_id_type=MESH
        )

    def load_own(n):
        ref = (k_ref, v_ref)[n // H] if n < 2 * H else q_ref
        h = n % H
        dst = KV.at[n // H, h, pl.ds(L, L)] if n < 2 * H else Q.at[h]
        return pltpu.make_async_copy(ref.at[:, pl.ds(h * HD, HD)], dst, l_sem.at[n])

    def load_w(s):
        return pltpu.make_async_copy(w_ref.at[:, pl.ds(s * CW, CW)], W.at[s], w_sem.at[s])

    load_g = pltpu.make_async_copy(g_ref, COT.at[hd], w_sem.at[4])
    for n in range(3 * H):
        load_own(n).start()
    load_g.start()
    for s in range(4):
        load_w(s).start()

    barrier = pltpu.get_barrier_semaphore()

    def greet(i, _):
        to = zl * NP + (t + i) % NP
        pl.semaphore_signal(barrier, inc=1, device_id=(to, hd), device_id_type=MESH)
        return 0

    lax.fori_loop(1, NP, greet, 0)
    pl.semaphore_signal(barrier, inc=1, device_id=((t + NP) % NT, hd), device_id_type=MESH)
    crossing = (NP, *Z_RELAY.values())
    for at in crossing:

        @pl.when(t == NP - 1)
        def _():
            pl.semaphore_signal(barrier, inc=1, device_id=(at, hd), device_id_type=MESH)

        @pl.when(t == at)
        def _():
            pl.semaphore_signal(barrier, inc=1, device_id=(NP - 1, hd), device_id_type=MESH)

    pl.semaphore_signal(barrier, inc=1, device_id=(t, mate), device_id_type=MESH)
    pl.semaphore_signal(barrier, inc=1, device_id=(t, far), device_id_type=MESH)
    met = jnp.where(t == NP - 1, len(crossing), 0)
    for at in crossing:
        met = met + jnp.where(t == at, 1, 0)
    pl.semaphore_wait(barrier, NP + 2 + met)

    row_end = (x == 3) & (y < 3)
    plane_end = t == NT // 2 - 1
    row_relay = (x == 3) & (y > 0)

    def kv_copies(n, h):
        src = (k_ref, v_ref)[n].at[:, pl.ds(h * HD, HD)]
        sem = kv_s.at[n, h]
        out = []
        direct = t < NT - 1
        if h >= 3:
            out.append((row_end, remote(src, RL.at[h - 3, n], sem, rl_r.at[h - 3, n], (t + 4, hd))))
            direct = direct & jnp.logical_not(row_end)
        if h in Z_RELAY:
            to = Z_RELAY[h]
            out.append((plane_end, remote(src, RL.at[0, n], sem, rl_r.at[0, n], (to, hd))))
            direct = direct & jnp.logical_not(plane_end)
        place = KV.at[n, h, pl.ds(0, L)]
        out.append((direct, remote(src, place, sem, kv_r.at[n, h], ((t + 1) % NT, hd))))
        return out

    def kv_relays():
        roles = [(row_relay, 0, 3, (t + NT - 3) % NT, 1), (row_relay, 1, 4, (t + NT - 3) % NT, 2)]
        roles += [(t == at, 0, h, NT // 2, h - 1) for h, at in Z_RELAY.items()]
        for mine, slot, h, to, turn in roles:
            for n in range(2):
                yield turn, mine, remote(
                    RL.at[slot, n], KV.at[n, h, pl.ds(0, L)], rl_s.at[slot, n], kv_r.at[n, h], (to, hd)
                ), remote(RL.at[slot, n], RL.at[slot, n], rl_s.at[slot, n], rl_r.at[slot, n], (to, hd))

    def when(condition, act):
        @pl.when(condition)
        def _():
            act()

    def zg_copy(r):
        rows = pl.ds(r * (L // GC), L // GC)
        return remote(g_ref.at[rows], COT.at[hd, rows], zg_s.at[r], zg_r.at[r], (t, far))

    def zg_wait(r):
        rows = pl.ds(r * (L // GC), L // GC)
        remote(COT.at[far, rows], COT.at[far, rows], zg_s.at[r], zg_r.at[r], (t, far)).wait_recv()

    def cf_copy(r):
        rows = pl.ds(r * (L // GC), L // GC)
        return remote(COT.at[far, rows], COT.at[far, rows], cf_s.at[r], cf_r.at[r], (t, mate))

    def cf_wait(r):
        rows = pl.ds(r * (L // GC), L // GC)
        remote(
            COT.at[far_mate, rows], COT.at[far_mate, rows], cf_s.at[r], cf_r.at[r], (t, mate)
        ).wait_recv()

    co_copy = remote(g_ref, COT.at[hd], co_s, co_r, (t, mate))
    co_arrival = remote(COT.at[mate], COT.at[mate], co_s, co_r, (t, mate))

    def send_kv(h, first):
        for n in range(2):
            copies = kv_copies(n, h)
            for condition, copy in copies[:-1] if first else copies[-1:]:
                when(condition, copy.start)

    co_copy.start()
    for r in range(EARLY_ZG):
        zg_copy(r).start()

    def piece(buf, i):
        i = i % NP
        return buf.at[i // 8, :, pl.ds(pl.multiple_of((i % 8) * 32, 32), 32), :]

    for n in range(3 * H):
        load_own(n).wait()

    @pl.when(t == 0)
    def _():
        for h in range(H):
            second = sink_ref[h].astype(F32)
            for n in range(2):
                a = KV[n, h, pl.ds(L, T)].astype(F32)
                b = KV[n, h, pl.ds(L + T, T)].astype(F32)
                RB[n, h] = (a * (1.0 - second) + b * second).astype(BF)
        SB[0, :, pl.ds(0, 32), :] = RB[0, :, pl.ds(0, 32), :]

        def scatter(i, _):
            remote(piece(RB, i), piece(SB, i), sc_s.at[i], sc_r, (i, hd)).start()
            return 0

        lax.fori_loop(1, NP, scatter, 0)

    @pl.when(t != 0)
    def _():
        remote(piece(SB, t), piece(SB, t), sc_s.at[1], sc_r, (0, hd)).wait_recv()

    over = remote(piece(SB, t), piece(SB, t), sc_s.at[0], sc_r, ((t + NP) % NT, hd))
    when(zl == 0, over.start)

    def ag_copy(i):
        to = zl * NP + (t + i) % NP
        return remote(piece(SB, t), piece(SB, t), ag_s.at[i], ag_r.at[t % NP], (to, hd))

    def ag_start(i, _):
        ag_copy(i).start()
        return 0

    lax.fori_loop(1, NP, ag_start, 0)
    for r in range(EARLY_ZG, GC):
        zg_copy(r).start()
    for h in (3, 4, 1, 2):
        send_kv(h, True)
    for h in range(H):
        send_kv(h, False)

    def use_rows(s, r, first=False):
        rows = pl.ds(pl.multiple_of(r * (L // GC), L // GC), L // GC)
        for half in range(2):
            turned = COT[s, rows, pl.ds(half * YB, YB)].T
            for i in range(4):
                COTT[2 * s + half, i, :, rows] = turned[i * XB : (i + 1) * XB]
        got = mmt(COT[s, rows], W[s])
        GA[rows] = got if first else GA[rows] + got

    def use_block(s, first):
        def body(r, _):
            use_rows(s, r, first)
            return 0

        lax.fori_loop(0, GC, body, 0)

    load_g.wait()
    for s in range(4):
        load_w(s).wait()
    use_block(hd, True)
    co_arrival.wait_recv()
    use_block(mate, False)

    def ag_wait(i, _):
        src = zl * NP + (t + i) % NP
        remote(piece(SB, src), piece(SB, src), ag_s.at[i], ag_r.at[src % NP], (src, hd)).wait_recv()
        return 0

    lax.fori_loop(1, NP, ag_wait, 0)

    @pl.when(t == 0)
    def _():
        KV[:, :, pl.ds(0, L)] = jnp.zeros((2, H, L, HD), BF)

    def biases(h, i):
        f = 2 * t + i
        win, snk = win_ref[h], sink_ref[h]
        off = jnp.float32(-1e30)
        on = jnp.float32(0.0)
        return (
            jnp.where((win >= 3) & (f >= 2), on, off),
            jnp.where((win >= 2) & (f >= 1), on, off),
            None,
            jnp.where(snk <= f - win, on, off),
        )

    def forward(h):
        vt = KV[1, h].T
        svt = SB[1, h].T
        for i in range(2):
            q = Q[h, pl.ds(i * T, T)]
            peak = None
            scores = []
            for b, bias in enumerate(biases(h, i)):
                keys = KV[0, h, pl.ds((i + b) * T, T)] if b < 3 else SB[0, h]
                s = mmt(keys, q) * SCALE2
                if bias is not None:
                    s = s + bias
                top = jnp.max(s, axis=0, keepdims=True)
                peak = top if peak is None else jnp.maximum(peak, top)
                scores.append(s)
            weights = [jnp.exp2(s - peak) for s in scores]
            total = sum(jnp.sum(e, axis=0, keepdims=True) for e in weights)
            inverse = 1.0 / total
            out = None
            for b, e in enumerate(weights):
                p = e * inverse
                PR[2 * h + i, pl.ds(b * T, T)] = p
                values = vt[:, (i + b) * T : (i + b + 1) * T] if b < 3 else svt
                term = mm(values, p.astype(BF))
                out = term if out is None else out + term
            ATT[h, :, pl.ds(i * T, T)] = out.astype(BF)

    row_start = (x == 0) & (y > 0)
    row_relay_back = (x == 0) & (y < 3)

    def d_direct(h):
        return remote(DPS.at[h], DPR.at[h], d_s.at[h], d_r.at[h], ((t + NT - 1) % NT, hd))

    def d_first(h):
        return remote(DPS.at[h], RLD.at[h - 3], d_s.at[h], rd_r.at[h - 3], ((t + NT - 4) % NT, hd))

    def d_onward(h):
        return remote(RLD.at[h - 3], DPR.at[h], rd_s.at[h - 3], d_r.at[h], ((t + 3) % NT, hd))

    def out_copy(n, h):
        ref = (dq_ref, dk_ref, dv_ref)[n]
        src = DQ.at[h] if n == 0 else DKV.at[n - 1, h]
        return pltpu.make_async_copy(src, ref.at[:, pl.ds(pl.multiple_of(h * HD, HD), HD)], o_sem.at[n, h])

    def backward(h):
        kt = KV[0, h].T
        skt = SB[0, h].T
        near = []
        for i in range(2):
            q = Q[h, pl.ds(i * T, T)]
            do = GA[pl.ds(i * T, T), pl.ds(pl.multiple_of(h * HD, HD), HD)].astype(BF)
            grads = []
            delta = None
            for b in range(4):
                values = KV[1, h, pl.ds((i + b) * T, T)] if b < 3 else SB[1, h]
                dp = mmt(values, do)
                term = jnp.sum(PR[2 * h + i, pl.ds(b * T, T)] * dp, axis=0, keepdims=True)
                delta = term if delta is None else delta + term
                grads.append(dp)
            out = None
            terms = []
            for b in range(4):
                p = PR[2 * h + i, pl.ds(b * T, T)]
                ds = (p * (grads[b] - delta) * SCALE).astype(BF)
                keys = kt[:, (i + b) * T : (i + b + 1) * T] if b < 3 else skt
                term = mm(keys, ds)
                out = term if out is None else out + term
                if b < 3:
                    terms.append((mm(ds, q), mm(p.astype(BF), do)))
            DQ[h, pl.ds(i * T, T)] = out.T.astype(BF)
            near.append(terms)
        out_copy(0, h).start()
        for n in range(2):
            DPS[h, n, pl.ds(0, T)] = near[0][0][n].astype(BF)
            DPS[h, n, pl.ds(T, T)] = (near[0][1][n] + near[1][0][n]).astype(BF)
            PR[2 * h, pl.ds(0, T), pl.ds(n * HD, HD)] = near[0][2][n] + near[1][1][n]
            PR[2 * h, pl.ds(T, T), pl.ds(n * HD, HD)] = near[1][2][n]
        when((t > 0) & jnp.logical_not(row_start & (h >= 3)), lambda: d_direct(h).start())
        when(row_start & (h >= 3), lambda: d_first(h).start())

    def finish_kv(h):
        @pl.when(t < NT - 1)
        def _():
            d_direct(h).wait_recv()

        @pl.when(t == NT - 1)
        def _():
            DPR[h] = jnp.zeros((2, L, HD), BF)

        for n in range(2):
            own = PR[2 * h, pl.ds(0, L), pl.ds(n * HD, HD)]
            DKV[n, h] = (own + DPR[h, n].astype(F32)).astype(BF)
            out_copy(n + 1, h).start()

    def which(j):
        h = j % H
        turned = (j >= H) & ((h == X_FIRST[0]) | (h == X_FIRST[1]))
        return (zh + j // H) % 2, h, turned, jnp.where(turned, x, y), jnp.where(turned, y, x)

    def way(j):
        return jnp.where((j < H) & (j != 3), -1, 1)

    def part(j, at):
        g, h, turned, _, _ = which(j)
        rows = jnp.concatenate(
            [COTT[g * 4 + jnp.where(turned, i, at), jnp.where(turned, at, i)] for i in range(4)]
        )
        return mmt(rows, ATT[h])

    def y_copy(j, m):
        _, _, turned, y1, _ = which(j)
        to = (y1 + (way(j) if m != 1 else -way(j)) + 4) % 4
        dev = zl * 16 + jnp.where(turned, y * 4 + to, to * 4 + x)
        return remote(YS.at[j, m], YR.at[j, m], y_s.at[j, m], y_r.at[j, m], (dev, hd))

    def x_copy(j, m):
        _, _, turned, _, x1 = which(j)
        to = (x1 + (way(j) if m != 1 else -way(j)) + 4) % 4
        dev = zl * 16 + jnp.where(turned, to * 4 + x, y * 4 + to)
        return remote(XS.at[j, m], XR.at[j, m], x_s.at[j, m], x_r.at[j, m], (dev, hd))

    def z_copy(h):
        return remote(ZS.at[h], ZR.at[h], z_s.at[h], z_r.at[h], ((t + 16) % NT, hd))

    def step1(j):
        y1 = which(j)[3]
        YS[j, 0] = part(j, (y1 + 2) % 4).astype(BF)
        y_copy(j, 0).start()
        YS[j, 1] = part(j, (y1 - way(j) + 4) % 4).astype(BF)
        y_copy(j, 1).start()

    def step2(j):
        own = part(j, (which(j)[3] + way(j) + 4) % 4)
        y_copy(j, 0).wait_recv()
        YS[j, 2] = (own + YR[j, 0].astype(F32)).astype(BF)
        y_copy(j, 2).start()

    def x_rows(xx):
        return pl.ds(pl.multiple_of(xx * XB, XB), XB)

    def step3(j):
        _, _, _, y1, x1 = which(j)
        own = part(j, y1)
        y_copy(j, 1).wait_recv()
        y_copy(j, 2).wait_recv()
        YSUM[...] = own + YR[j, 1].astype(F32) + YR[j, 2].astype(F32)
        XS[j, 0] = YSUM[x_rows((x1 + 2) % 4)].astype(BF)
        x_copy(j, 0).start()
        XS[j, 1] = YSUM[x_rows((x1 - way(j) + 4) % 4)].astype(BF)
        x_copy(j, 1).start()
        XK[j, 0] = YSUM[x_rows((x1 + way(j) + 4) % 4)]
        XK[j, 1] = YSUM[x_rows(x1)]

    def step4(j):
        x_copy(j, 0).wait_recv()
        XS[j, 2] = (XK[j, 0] + XR[j, 0].astype(F32)).astype(BF)
        x_copy(j, 2).start()

    def step5(j):
        g, h, _, _, _ = which(j)
        x_copy(j, 1).wait_recv()
        x_copy(j, 2).wait_recv()
        ZF[g, h] = XK[j, 1] + XR[j, 1].astype(F32) + XR[j, 2].astype(F32)

        @pl.when(j >= H)
        def _():
            ZS[h] = ZF[1 - zl, h].astype(BF)
            z_copy(h).start()

    def step6(h):
        z_copy(h).wait_recv()
        at = pl.ds(pl.multiple_of(h * HD, HD), HD)
        WO[at] = (ZF[zl, h] + ZR[h].astype(F32)).T

    def turn(j, _):
        for at, mine, onward, arrival in kv_relays():
            when(mine & (j == at), arrival.wait_recv)
            when(mine & (j == at), onward.start)

        @pl.when((j >= 2) & (j < GC + 2))
        def _():
            cf_wait(j - 2)
            use_rows(far_mate, j - 2)

        @pl.when(j < H)
        def _():
            @pl.when(t > 0)
            def _():
                for n in range(2):
                    place = KV.at[n, j, pl.ds(0, L)]
                    remote(place, place, kv_s.at[n, j], kv_r.at[n, j], ((t + 1) % NT, hd)).wait_recv()

            forward(j)

        @pl.when(j < 2 * H)
        def _():
            step1(j)

        @pl.when((j >= LAG2) & (j < 2 * H + LAG2))
        def _():
            step2(j - LAG2)

        @pl.when((j >= 1) & (j < GC + 1))
        def _():
            zg_wait(j - 1)
            cf_copy(j - 1).start()
            use_rows(far, j - 1)

        @pl.when((j >= H) & (j < 2 * H))
        def _():
            backward(j - H)

        @pl.when((j >= LAG3) & (j < 2 * H + LAG3))
        def _():
            step3(j - LAG3)

        @pl.when((j >= LAG4) & (j < 2 * H + LAG4))
        def _():
            step4(j - LAG4)

        @pl.when(row_relay_back & (j >= 2 * H) & (j < 2 * H + 2))
        def _():
            h = j - 2 * H + 3
            remote(RLD.at[h - 3], RLD.at[h - 3], rd_s.at[h - 3], rd_r.at[h - 3], (t, hd)).wait_recv()
            d_onward(h).start()

        @pl.when((j >= H + 5) & (j < 2 * H + 5))
        def _():
            finish_kv(j - H - 5)

        @pl.when((j >= LAG5) & (j < 2 * H + LAG5))
        def _():
            step5(j - LAG5)

        @pl.when(j >= H + LAG6)
        def _():
            step6(j - H - LAG6)

        return 0

    lax.fori_loop(0, 2 * H + LAG6, turn, 0)
    put_w = pltpu.make_async_copy(WO, wo_ref, w_sem.at[4])
    put_w.start()

    when(zl == 0, over.wait_send)
    co_copy.wait_send()
    for r in range(GC):
        zg_copy(r).wait_send()
        cf_copy(r).wait_send()

    @pl.when(t == 0)
    def _():
        def sent(i, _):
            remote(piece(RB, i), piece(SB, i), sc_s.at[i], sc_r, (i, hd)).wait_send()
            return 0

        lax.fori_loop(1, NP, sent, 0)

    def ag_sent(i, _):
        ag_copy(i).wait_send()
        return 0

    lax.fori_loop(1, NP, ag_sent, 0)

    def rs_sent(j, _):
        for m in range(3):
            y_copy(j, m).wait_send()
            x_copy(j, m).wait_send()
        return 0

    lax.fori_loop(0, 2 * H, rs_sent, 0)
    for h in range(H):
        for n in range(2):
            for condition, copy in kv_copies(n, h):
                when(condition, copy.wait_send)
        z_copy(h).wait_send()
        when(t > 0, d_direct(h).wait_send)
        for n in range(3):
            out_copy(n, h).wait()
    for _, mine, onward, _ in kv_relays():
        when(mine, onward.wait_send)
    for h in (3, 4):
        when(row_relay_back, d_onward(h).wait_send)
    put_w.wait()


def hand_over(a, b, c, d, a_out, b_out, c_out, d_out, a_mid, b_mid, c_mid, d_mid, sem):
    arrays = ((a, a_mid, a_out), (b, b_mid, b_out), (c, c_mid, c_out), (d, d_mid, d_out))
    copies = [
        (pltpu.make_async_copy(src, mid, sem.at[0, i]), pltpu.make_async_copy(mid, dst, sem.at[1, i]))
        for i, (src, mid, dst) in enumerate(arrays)
    ]
    for load, _ in copies:
        load.start()
    for load, store in copies:
        load.wait()
        store.start()
    for _, store in copies:
        store.wait()


def per_device(query, key, value, out_weight, grad_out, sink_frame, window):
    dma = pltpu.SemaphoreType.DMA
    any_spec = pl.BlockSpec(memory_space=pl.ANY)
    smem = pl.BlockSpec(memory_space=pltpu.SMEM)
    sds = jax.ShapeDtypeStruct
    grad_query, grad_key, grad_value, weight = pl.pallas_call(
        kernel,
        out_shape=[sds((L, H * HD), BF)] * 3 + [sds((H * HD, XB), F32)],
        in_specs=[any_spec] * 5 + [smem] * 2,
        out_specs=[any_spec] * 4,
        scratch_shapes=[
            pltpu.VMEM((H, L, HD), BF),
            pltpu.VMEM((2, H, 2 * L, HD), BF),
            pltpu.VMEM((2, H, T, HD), BF),
            pltpu.VMEM((2, H, T, HD), BF),
            pltpu.VMEM((2, 2, L, HD), BF),
            pltpu.VMEM((2, 2, L, HD), BF),
            pltpu.VMEM((4, L, CW), BF),
            pltpu.VMEM((8, 4, XB, L), BF),
            pltpu.VMEM((4, H * HD, CW), BF),
            pltpu.VMEM((L, H * HD), F32),
            pltpu.VMEM((2 * H, 4 * T, T), F32),
            pltpu.VMEM((H, HD, L), BF),
            pltpu.VMEM((2 * H, 3, YB, HD), BF),
            pltpu.VMEM((2 * H, 3, YB, HD), BF),
            pltpu.VMEM((YB, HD), F32),
            pltpu.VMEM((2 * H, 3, XB, HD), BF),
            pltpu.VMEM((2 * H, 3, XB, HD), BF),
            pltpu.VMEM((2 * H, 2, XB, HD), F32),
            pltpu.VMEM((2, H, XB, HD), F32),
            pltpu.VMEM((H, XB, HD), BF),
            pltpu.VMEM((H, XB, HD), BF),
            pltpu.VMEM((H * HD, XB), F32),
            pltpu.VMEM((H, 2, L, HD), BF),
            pltpu.VMEM((H, 2, L, HD), BF),
            pltpu.VMEM((H, L, HD), BF),
            pltpu.VMEM((2, H, L, HD), BF),
            dma((3 * H,)), dma((5,)),
            dma((2, H)), dma((2, H)), dma((2, 2)), dma((2, 2)), dma((2,)), dma((2,)),
            dma((GC,)), dma((GC,)),
            dma, dma,
            dma((GC,)), dma((GC,)),
            dma((NT,)), dma,
            dma((NP,)), dma((NP,)),
            dma((2 * H, 3)), dma((2 * H, 3)),
            dma((2 * H, 3)), dma((2 * H, 3)),
            dma((H,)), dma((H,)),
            dma((H,)), dma((H,)),
            dma((3, H)),
        ],
        compiler_params=pltpu.CompilerParams(
            collective_id=0, has_side_effects=True, vmem_limit_bytes=60 * 1024 * 1024
        ),
        name="layer_backward",
    )(query, key, value, out_weight, grad_out, sink_frame, window)
    outs = [sds((L, H * HD), BF)] * 3 + [sds((H * HD, XB), F32)]
    return tuple(
        pl.pallas_call(
            hand_over,
            out_shape=outs,
            in_specs=[any_spec] * 4,
            out_specs=[any_spec] * 4,
            scratch_shapes=[pltpu.VMEM(o.shape, o.dtype) for o in outs] + [dma((2, 4))],
            compiler_params=pltpu.CompilerParams(vmem_limit_bytes=60 * 1024 * 1024),
            name="hand_over",
        )(grad_query, grad_key, grad_value, weight)
    )


def solution(mesh):
    placed = (
        P("tm", "head"),
        P("tm", "head"),
        P("tm", "head"),
        P("head", None),
        P("tm", "head"),
        P("head"),
        P("head"),
    )
    return jax.shard_map(
        per_device,
        mesh=mesh,
        in_specs=placed,
        out_specs=(P("tm", "head"), P("tm", "head"), P("tm", "head"), P("head", "tm")),
        check_vma=False,
    )
```
